512 devices in a mesh: dp: 4 (over y_lo, core), tensor: 4 (over x), context: 32 (over y_hi, z).
Axes of the slice: x: 4, y: 8 (y_hi: 4, y_lo: 2; y = y_hi * 2 + y_lo), z: 8, core: 2. Of those that a mesh axis runs over, the one named last changes fastest.
Arguments:
- inputs: bfloat16 [4, 4096, 4096], P('dp', 'context', 'tensor'), may hold values from -6 to 6
- value_weight: bfloat16 [4096, 4096], P(('tensor', 'context')), may hold values from -0.09375 to 0.09375
- query: bfloat16 [4, 4096, 4096], P('dp', 'tensor', 'context'), may hold values from -6 to 6
- key: bfloat16 [4, 4096, 4096], P('dp', 'tensor', 'context'), may hold values from -6 to 6
- filters: float32 [4096, 4096], P(('tensor', 'context')), may hold values from -5 to 5
- skip: float32 [4096], P(('tensor', 'context')), may hold values from 0.1 to 1.9
- cotangent: bfloat16 [4, 4096, 4096], P('dp', 'tensor', 'context'), may hold values from -6 to 6
Outputs:
- gated: bfloat16 [4, 4096, 4096], P('dp', 'tensor', 'context')
- query_grad: bfloat16 [4, 4096, 4096], P('dp', 'tensor', 'context')
- key_grad: bfloat16 [4, 4096, 4096], P('dp', 'tensor', 'context')
- input_grad: bfloat16 [4, 4096, 4096], P('dp', 'context', 'tensor')
- filter_grad: float32 [4096, 4096], P(('tensor', 'context'))
- skip_grad: float32 [4096], P(('tensor', 'context'))
The draws below stay inside these ranges and needn't reach their ends.
All inputs are finite; a program needn't handle non-finite values.
Results may differ from the reference program's by a relative error of at most 0.018.
Values may be sent and summed in bfloat16 or wider, within the bound.
No kernel may reach another device: no remote copies, remote signals or barrier semaphores. Data moves between devices by JAX's collectives and lax.ppermute only.
A program may use at most 64 MiB of HBM per device.

```python
import math
import jax
import jax.numpy as jnp
from jax import lax

D = 4096
C = 4096
SEQ = 4096
BATCH = 4


def draw_filters(key, part):
    key = jax.random.fold_in(key, 7)
    span_key, noise_key = jax.random.split(key, 2)
    lags = jnp.arange(SEQ, dtype=jnp.float32)[None, :]
    log_span = jax.random.uniform(span_key, (C, 1), jnp.float32, math.log(40.0), math.log(2.0 * SEQ))
    noise = jax.random.truncated_normal(noise_key, -5.0, 5.0, (C, SEQ), jnp.float32)
    spans = jnp.exp(log_span)
    rate = jnp.exp(-1.0 / spans)
    scale = jnp.sqrt((1.0 - rate * rate) / (1.0 - jnp.exp(-2.0 * SEQ / spans)))
    decay = jnp.exp(-lags / spans)
    return (scale * decay * noise).astype(jnp.float32)


def level_of(stream_key, dims, cuts, low, largest):
    factor_of, own = 1.0, jax.random.fold_in(stream_key, 6)
    for dim, shards_of in cuts:
        heights = jnp.exp(jax.random.uniform(jax.random.fold_in(own, dim), (shards_of,), jnp.float32, low / len(cuts), largest / len(cuts)))
        factor_of = factor_of * jnp.repeat(heights, dims[dim] // shards_of).reshape([-1 if axis == dim else 1 for axis in range(len(dims))])
    return factor_of


def bell_draw(key, dims, width, bound, cuts=(), held_as=jnp.bfloat16):
    entries = width * jax.random.normal(key, dims, jnp.float32)
    if cuts:
        entries = entries * level_of(key, dims, cuts, -0.22, 0.18)
    return jnp.clip(entries, -bound, bound).astype(held_as)


def setup_inputs(seed: int = 0) -> dict:
    keys = jax.random.split(jax.random.key(seed), 8)
    return {
        "inputs": bell_draw(keys[0], (BATCH, SEQ, D), 1.0, 6.0, ((0, 4), (1, 32), (2, 4))),
        "value_weight": bell_draw(keys[1], (D, C), D ** -0.5, 0.09375, ((0, 128),)),
        "query": bell_draw(keys[2], (BATCH, C, SEQ), 1.0, 6.0, ((0, 4), (1, 4), (2, 32))),
        "key": bell_draw(keys[3], (BATCH, C, SEQ), 1.0, 6.0, ((0, 4), (1, 4), (2, 32))),
        "filters": draw_filters(jax.random.fold_in(keys[7], 71), 0),
        "skip": jnp.clip(1.0 + 0.18 * jax.random.normal(keys[5], (C,), jnp.float32), 0.1, 1.9),
        "cotangent": bell_draw(keys[6], (BATCH, C, SEQ), 1.0, 6.0, ((0, 4), (1, 4), (2, 32))),
    }


def one_sequence(operands, value_weight, filters, skip):
    tokens, query_in, key_in, grad_out = operands
    value_rows = jnp.dot(tokens, value_weight, preferred_element_type=jnp.float32).astype(jnp.bfloat16)
    value_part = value_rows.T.astype(jnp.float32)
    query_part = query_in.astype(jnp.float32)
    key_part = key_in.astype(jnp.float32)
    mix = (key_part * value_part).astype(jnp.bfloat16).astype(jnp.float32)
    fft_size = 2 * SEQ
    filter_spec = jnp.fft.rfft(filters, fft_size, axis=1)
    mix_spec = jnp.fft.rfft(mix, fft_size, axis=1)
    conv_full = jnp.fft.irfft(filter_spec * mix_spec, fft_size, axis=1)[:, :SEQ]
    conv = (conv_full + skip[:, None] * mix).astype(jnp.bfloat16).astype(jnp.float32)
    gated = (query_part * conv).astype(jnp.bfloat16)
    upstream = grad_out.astype(jnp.float32)
    dconv = (upstream * query_part).astype(jnp.bfloat16).astype(jnp.float32)
    query_grad = (upstream * conv).astype(jnp.bfloat16)
    grad_spec = jnp.fft.rfft(dconv, fft_size, axis=1)
    dmix_full = jnp.fft.irfft(jnp.conj(filter_spec) * grad_spec, fft_size, axis=1)[:, :SEQ]
    dmix = (dmix_full + skip[:, None] * dconv).astype(jnp.bfloat16).astype(jnp.float32)
    filter_term = jnp.fft.irfft(jnp.conj(mix_spec) * grad_spec, fft_size, axis=1)[:, :SEQ]
    skip_term = jnp.sum(dconv * mix, axis=1)
    key_grad = (dmix * value_part).astype(jnp.bfloat16)
    dvalue = (dmix * key_part).astype(jnp.bfloat16)
    input_grad = jnp.dot(dvalue.T, value_weight.T, preferred_element_type=jnp.float32).astype(jnp.bfloat16)
    return gated, query_grad, key_grad, input_grad, filter_term.astype(jnp.float32), skip_term.astype(jnp.float32)


def reference(inputs, value_weight, query, key, filters, skip, cotangent):
    results = lax.map(lambda operands: one_sequence(operands, value_weight, filters, skip), (inputs, query, key, cotangent))
    gated, query_grad, key_grad, input_grad, filter_terms, skip_terms = results
    return gated, query_grad, key_grad, input_grad, jnp.sum(filter_terms, axis=0), jnp.sum(skip_terms, axis=0)
```

```python
import jax
import jax.numpy as jnp
from jax import lax
from jax.experimental import pallas as pl
from jax.experimental.pallas import tpu as pltpu
from jax.sharding import PartitionSpec as P

f32 = jnp.float32
bf16 = jnp.bfloat16

LANES = 128
GROUP = 8
SEQS = 4
BLOCKS = 32
ROWS = BLOCKS * SEQS
SIGNAL = ROWS * GROUP
TAPS = BLOCKS * LANES
WIDE = TAPS + LANES


def load_pair(pair_ref):
    both = pair_ref[...].astype(f32).reshape(ROWS, 2, GROUP, LANES)
    return both[:, 0].reshape(SIGNAL, LANES), both[:, 1].reshape(SIGNAL, LANES)


def early_kernel(filters_ref, skip_ref, pair_ref, dmix_ref, dvalue_ref, taps_ref, rolled, grads, ahead, wide, result):
    chan = pl.program_id(0)

    @pl.when(chan == 0)
    def _():
        dconv, _ = load_pair(pair_ref)
        grads[0:SIGNAL, :] = dconv
        grads[SIGNAL:, :] = jnp.zeros((SIGNAL, LANES), f32)
        padded = jnp.concatenate([filters_ref[...], jnp.zeros((GROUP, LANES), f32)], axis=1)
        for row in range(GROUP):
            turned = pltpu.roll(padded, row, 1) if row else padded
            for block in range(BLOCKS + 1):
                rolled[block, row * GROUP : (row + 1) * GROUP, :] = turned[:, block * LANES : (block + 1) * LANES]

    base = jnp.concatenate(
        [rolled[block, pl.ds(chan, GROUP, stride=GROUP), :] for block in range(BLOCKS + 1)], axis=1
    )
    for pair in range(LANES // 16):
        low = pltpu.roll(base, 16 * pair, 1) if pair else base
        high = pltpu.roll(base, 16 * pair + 8, 1)
        tile = jnp.concatenate([low[:, :TAPS], high[:, :TAPS]], axis=0).astype(bf16)
        wide[16 * pair : 16 * pair + 16, :] = tile
        for block in range(BLOCKS):
            taps_ref[0, block * LANES + 16 * pair : block * LANES + 16 * pair + 16, :] = tile[
                :, block * LANES : (block + 1) * LANES
            ]
    for block in range(BLOCKS):
        ahead[:, block * LANES : (block + 1) * LANES] = grads[
            pl.ds(block * SEQS * GROUP + chan, ROWS, stride=GROUP), :
        ].astype(bf16)
    total = lax.dot_general(ahead[...], wide[...], (((1,), (1,)), ((), ())), preferred_element_type=f32)
    own = grads[pl.ds(chan, ROWS, stride=GROUP), :]
    result[pl.ds(chan, ROWS, stride=GROUP), :] = total + skip_ref[chan] * own

    @pl.when(chan == GROUP - 1)
    def _():
        _, key = load_pair(pair_ref)
        dmix = result[...].astype(bf16)
        dmix_ref[...] = dmix
        dvalue = (dmix.astype(f32) * key).reshape(BLOCKS, SEQS, GROUP, LANES)
        for seq in range(SEQS):
            dvalue_ref[:, seq * LANES : (seq + 1) * LANES] = (
                dvalue[:, seq].reshape(BLOCKS * GROUP, LANES).astype(bf16)
            )


def late_kernel(taps_ref, skip_ref, pair_ref, value_ref, dmix_ref, out_ref, fgrad_ref, mixes, grads, behind, ahead, corr, sums, result, kgrad):
    chan = pl.program_id(0)

    @pl.when(chan == 0)
    def _():
        dconv, key = load_pair(pair_ref)
        grads[0:SIGNAL, :] = dconv
        grads[SIGNAL:, :] = jnp.zeros((SIGNAL, LANES), f32)
        value = value_ref[...].astype(f32)
        parts = [
            value[:, seq * LANES : (seq + 1) * LANES].reshape(BLOCKS, 1, GROUP, LANES) for seq in range(SEQS)
        ]
        value = jnp.concatenate(parts, axis=1).reshape(SIGNAL, LANES)
        mixes[0:SIGNAL, :] = jnp.zeros((SIGNAL, LANES), f32)
        mixes[SIGNAL:, :] = (key * value).astype(bf16).astype(f32)
        kgrad[...] = dmix_ref[...].astype(f32) * value
        corr[:, TAPS:] = jnp.zeros((LANES, LANES), f32)

    for block in range(BLOCKS):
        lanes = slice(block * LANES, (block + 1) * LANES)
        behind[:, lanes] = mixes[pl.ds(SIGNAL - block * SEQS * GROUP + chan, ROWS, stride=GROUP), :].astype(bf16)
        ahead[:, lanes] = grads[pl.ds(block * SEQS * GROUP + chan, ROWS, stride=GROUP), :].astype(bf16)
    own = mixes[pl.ds(SIGNAL + chan, ROWS, stride=GROUP), :]
    total = jnp.dot(behind[...], taps_ref[0], preferred_element_type=f32)
    result[pl.ds(chan, ROWS, stride=GROUP), :] = total + skip_ref[chan] * own
    corr[:, :TAPS] = jnp.dot(own.T.astype(bf16), ahead[...], preferred_element_type=f32)
    acc = corr[0:GROUP, :]
    for group in range(1, LANES // GROUP):
        acc = acc + pltpu.roll(corr[group * GROUP : (group + 1) * GROUP, :], WIDE - group * GROUP, 1)
    for block in range(BLOCKS + 1):
        sums[block, pl.ds(pl.multiple_of(chan * GROUP, GROUP), GROUP), :] = acc[:, block * LANES : (block + 1) * LANES]

    @pl.when(chan == GROUP - 1)
    def _():
        both = [
            result[...].reshape(ROWS, 1, GROUP, LANES),
            kgrad[...].reshape(ROWS, 1, GROUP, LANES),
        ]
        out_ref[...] = jnp.concatenate(both, axis=1).reshape(2 * SIGNAL, LANES).astype(bf16)
        fgrad = None
        for row in range(GROUP):
            part = jnp.concatenate(
                [sums[block, pl.ds(row, GROUP, stride=GROUP), :] for block in range(BLOCKS + 1)], axis=1
            )
            fgrad = part if row == 0 else fgrad + pltpu.roll(part, WIDE - row, 1)
        fgrad_ref[...] = fgrad[:, :TAPS].astype(bf16)


def whole(shape):
    return pl.BlockSpec(shape, lambda chan: (0,) * len(shape))


params = pltpu.CompilerParams(vmem_limit_bytes=48 * 1024 * 1024)
smem = pl.BlockSpec(memory_space=pltpu.SMEM)
taps_spec = pl.BlockSpec((1, TAPS, LANES), lambda chan: (chan, 0, 0))


def early(filters, skip, pair):
    return pl.pallas_call(
        early_kernel,
        grid=(GROUP,),
        in_specs=[whole((GROUP, TAPS)), smem, whole((2 * SIGNAL, LANES))],
        out_specs=[whole((SIGNAL, LANES)), whole((BLOCKS * GROUP, SEQS * LANES)), taps_spec],
        out_shape=[
            jax.ShapeDtypeStruct((SIGNAL, LANES), bf16),
            jax.ShapeDtypeStruct((BLOCKS * GROUP, SEQS * LANES), bf16),
            jax.ShapeDtypeStruct((GROUP, TAPS, LANES), bf16),
        ],
        scratch_shapes=[
            pltpu.VMEM((BLOCKS + 1, GROUP * GROUP, LANES), f32),
            pltpu.VMEM((2 * SIGNAL, LANES), f32),
            pltpu.VMEM((ROWS, TAPS), bf16),
            pltpu.VMEM((LANES, TAPS), bf16),
            pltpu.VMEM((SIGNAL, LANES), f32),
        ],
        compiler_params=params,
        name="early",
    )(filters, skip, pair)


def late(taps, skip, pair, value, dmix):
    return pl.pallas_call(
        late_kernel,
        grid=(GROUP,),
        in_specs=[
            taps_spec,
            smem,
            whole((2 * SIGNAL, LANES)),
            whole((BLOCKS * GROUP, SEQS * LANES)),
            whole((SIGNAL, LANES)),
        ],
        out_specs=[whole((2 * SIGNAL, LANES)), whole((GROUP, TAPS))],
        out_shape=[
            jax.ShapeDtypeStruct((2 * SIGNAL, LANES), bf16),
            jax.ShapeDtypeStruct((GROUP, TAPS), bf16),
        ],
        scratch_shapes=[
            pltpu.VMEM((2 * SIGNAL, LANES), f32),
            pltpu.VMEM((2 * SIGNAL, LANES), f32),
            pltpu.VMEM((ROWS, TAPS), bf16),
            pltpu.VMEM((ROWS, TAPS), bf16),
            pltpu.VMEM((LANES, WIDE), f32),
            pltpu.VMEM((BLOCKS + 1, GROUP * GROUP, LANES), f32),
            pltpu.VMEM((SIGNAL, LANES), f32),
            pltpu.VMEM((SIGNAL, LANES), f32),
        ],
        compiler_params=params,
        name="late",
    )(taps, skip, pair, value, dmix)


def swap(values, axes):
    return lax.all_to_all(values, axes, split_axis=0, concat_axis=0, tiled=True)


def pick_columns(weight, quarter):
    span = 512
    source = lax.broadcasted_iota(jnp.int32, (span, LANES), 0)
    target = lax.broadcasted_iota(jnp.int32, (span, LANES), 1)
    chosen = (source == (target // GROUP) * (GROUP * SEQS) + quarter * GROUP + target % GROUP).astype(bf16)
    parts = [
        jnp.dot(weight[:, start : start + span], chosen, preferred_element_type=f32).astype(bf16)
        for start in range(0, weight.shape[1], span)
    ]
    return jnp.concatenate(parts, axis=1)


def per_device(inputs, value_weight, query, key, filters, skip, cotangent):
    quarter = lax.axis_index("dp")
    rows = value_weight.shape[0]
    picked = pick_columns(value_weight, quarter)
    half = picked.shape[1] // 2
    halves = [
        swap(jnp.broadcast_to(part[None], (BLOCKS,) + part.shape), "context").reshape(BLOCKS * rows, half)
        for part in (picked[:, :half], picked[:, half:])
    ]
    tokens = lax.all_gather(inputs[0], "dp", axis=0, tiled=True)

    query_part = query[0].astype(f32)
    upstream = cotangent[0].astype(f32)
    dconv = (upstream * query_part).astype(bf16)
    pair = jnp.concatenate([dconv.reshape(ROWS, 1, GROUP, LANES), key[0].reshape(ROWS, 1, GROUP, LANES)], axis=1)
    pair = swap(pair, ("context", "dp")).reshape(2 * SIGNAL, LANES)
    own_filters = lax.dynamic_slice_in_dim(filters, quarter * GROUP, GROUP, 0)
    own_skip = lax.dynamic_slice_in_dim(skip, quarter * GROUP, GROUP, 0)
    dmix, dvalue, taps = early(own_filters, own_skip, pair)
    dvalue = swap(dvalue.reshape(BLOCKS, GROUP, SEQS * LANES), "context").reshape(BLOCKS * GROUP, SEQS * LANES)
    dvalue = lax.all_gather(dvalue, "tensor", axis=0, tiled=True)

    weight = jnp.concatenate(halves, axis=1)
    partial = lax.dot_general(weight, tokens, (((0,), (1,)), ((), ())), preferred_element_type=f32).astype(bf16)
    partial = swap(partial.reshape(4, BLOCKS * GROUP, SEQS * LANES), "tensor").astype(f32)
    value = (partial[0] + partial[1] + partial[2] + partial[3]).astype(bf16)
    value = swap(value.reshape(BLOCKS, GROUP, SEQS * LANES), "context").reshape(BLOCKS * GROUP, SEQS * LANES)
    out, fgrad = late(taps, own_skip, pair, value, dmix)
    out = swap(out.reshape(ROWS, 2, GROUP, LANES), ("context", "dp"))
    conv = out[:, 0].reshape(SIGNAL, LANES).astype(f32)
    key_grad = out[:, 1].reshape(SIGNAL, LANES)
    gated = (query_part * conv).astype(bf16)
    query_grad = (upstream * conv).astype(bf16)
    filter_grad = lax.all_gather(fgrad, "dp", axis=0, tiled=True).astype(f32)
    skip_grad = filter_grad[:, 0]

    grad = lax.dot_general(dvalue, weight, (((0,), (1,)), ((), ())), preferred_element_type=f32).astype(bf16)
    grad = swap(grad.reshape(SEQS, LANES, grad.shape[1]), "dp").astype(f32)
    input_grad = (grad[0] + grad[1] + grad[2] + grad[3]).astype(bf16)
    return (gated[None], query_grad[None], key_grad[None], input_grad[None], filter_grad, skip_grad)


def solution(mesh):
    by_channel = P("dp", "tensor", "context")
    by_row = P(("tensor", "context"), None)
    in_specs = (
        P("dp", "context", "tensor"),
        by_row,
        by_channel,
        by_channel,
        by_row,
        P(("tensor", "context")),
        by_channel,
    )
    out_specs = (
        by_channel,
        by_channel,
        by_channel,
        P("dp", "context", "tensor"),
        by_row,
        P(("tensor", "context")),
    )
    return jax.shard_map(
        per_device, mesh=mesh, in_specs=in_specs, out_specs=out_specs, check_vma=False
    )
```

```python
import jax
import jax.numpy as jnp
from jax import lax
from jax.experimental import pallas as pl
from jax.experimental.pallas import tpu as pltpu
from jax.sharding import PartitionSpec as P

f32 = jnp.float32
bf16 = jnp.bfloat16

LANES = 128
GROUP = 8
SEQS = 4
BLOCKS = 32
ROWS = BLOCKS * SEQS
SIGNAL = ROWS * GROUP
TAPS = BLOCKS * LANES
WIDE = TAPS + LANES


def load_pair(pair_ref):
    both = pair_ref[...].astype(f32).reshape(ROWS, 2, GROUP, LANES)
    return both[:, 0].reshape(SIGNAL, LANES), both[:, 1].reshape(SIGNAL, LANES)


def early_kernel(filters_ref, skip_ref, pair_ref, dmix_ref, dvalue_ref, taps_ref, rolled, grads, ahead, wide, result):
    chan = pl.program_id(0)

    @pl.when(chan == 0)
    def _():
        dconv, _ = load_pair(pair_ref)
        grads[0:SIGNAL, :] = dconv
        grads[SIGNAL:, :] = jnp.zeros((SIGNAL, LANES), f32)
        padded = jnp.concatenate([filters_ref[...], jnp.zeros((GROUP, LANES), f32)], axis=1)
        for row in range(GROUP):
            turned = pltpu.roll(padded, row, 1) if row else padded
            for block in range(BLOCKS + 1):
                rolled[block, row * GROUP : (row + 1) * GROUP, :] = turned[:, block * LANES : (block + 1) * LANES]

    base = jnp.concatenate(
        [rolled[block, pl.ds(chan, GROUP, stride=GROUP), :] for block in range(BLOCKS + 1)], axis=1
    )
    for pair in range(LANES // 16):
        low = pltpu.roll(base, 16 * pair, 1) if pair else base
        high = pltpu.roll(base, 16 * pair + 8, 1)
        tile = jnp.concatenate([low[:, :TAPS], high[:, :TAPS]], axis=0).astype(bf16)
        wide[16 * pair : 16 * pair + 16, :] = tile
        for block in range(BLOCKS):
            taps_ref[0, block * LANES + 16 * pair : block * LANES + 16 * pair + 16, :] = tile[
                :, block * LANES : (block + 1) * LANES
            ]
    for block in range(BLOCKS):
        ahead[:, block * LANES : (block + 1) * LANES] = grads[
            pl.ds(block * SEQS * GROUP + chan, ROWS, stride=GROUP), :
        ].astype(bf16)
    total = lax.dot_general(ahead[...], wide[...], (((1,), (1,)), ((), ())), preferred_element_type=f32)
    own = grads[pl.ds(chan, ROWS, stride=GROUP), :]
    result[pl.ds(chan, ROWS, stride=GROUP), :] = total + skip_ref[chan] * own

    @pl.when(chan == GROUP - 1)
    def _():
        _, key = load_pair(pair_ref)
        dmix = result[...].astype(bf16)
        dmix_ref[...] = dmix
        dvalue = (dmix.astype(f32) * key).reshape(BLOCKS, SEQS, GROUP, LANES)
        for seq in range(SEQS):
            dvalue_ref[:, seq * LANES : (seq + 1) * LANES] = (
                dvalue[:, seq].reshape(BLOCKS * GROUP, LANES).astype(bf16)
            )


def conv_kernel(taps_ref, skip_ref, place_ref, pair_ref, value_ref, dmix_ref, out_ref, mix_ref, mixes, values, behind, result):
    chan = pl.program_id(0)

    @pl.when(chan == 0)
    def _():
        _, key = load_pair(pair_ref)
        for piece in range(2 * SEQS):
            core, high, side = piece // 4, piece // 2 % 2, piece % 2
            seq = (high ^ place_ref[1]) * 2 + (core ^ place_ref[2])
            start = (side ^ place_ref[0]) * (SEQS * GROUP) + seq * GROUP
            part = value_ref[:, piece * LANES : (piece + 1) * LANES].astype(f32)
            for two in range(BLOCKS // 2):
                row = pl.multiple_of(two * (2 * SEQS * GROUP) + start, GROUP)
                values[pl.ds(row, GROUP), :] = part[two * GROUP : (two + 1) * GROUP, :]
        mix = (key * values[...]).astype(bf16)
        mix_ref[...] = mix
        mixes[0:SIGNAL, :] = jnp.zeros((SIGNAL, LANES), f32)
        mixes[SIGNAL:, :] = mix.astype(f32)

    for block in range(BLOCKS):
        behind[:, block * LANES : (block + 1) * LANES] = mixes[
            pl.ds(SIGNAL - block * SEQS * GROUP + chan, ROWS, stride=GROUP), :
        ].astype(bf16)
    own = mixes[pl.ds(SIGNAL + chan, ROWS, stride=GROUP), :]
    total = jnp.dot(behind[...], taps_ref[0], preferred_element_type=f32)
    result[pl.ds(chan, ROWS, stride=GROUP), :] = total + skip_ref[chan] * own

    @pl.when(chan == GROUP - 1)
    def _():
        kgrad = dmix_ref[...].astype(f32) * values[...]
        both = [result[...].reshape(ROWS, 1, GROUP, LANES), kgrad.reshape(ROWS, 1, GROUP, LANES)]
        out_ref[...] = jnp.concatenate(both, axis=1).reshape(2 * SIGNAL, LANES).astype(bf16)


def fgrad_kernel(pair_ref, mix_ref, fgrad_ref, mixes, grads, ahead, corr, sums):
    chan = pl.program_id(0)

    @pl.when(chan == 0)
    def _():
        dconv, _ = load_pair(pair_ref)
        grads[0:SIGNAL, :] = dconv
        grads[SIGNAL:, :] = jnp.zeros((SIGNAL, LANES), f32)
        mixes[...] = mix_ref[...].astype(f32)
        corr[:, TAPS:] = jnp.zeros((LANES, LANES), f32)

    for block in range(BLOCKS):
        ahead[:, block * LANES : (block + 1) * LANES] = grads[
            pl.ds(block * SEQS * GROUP + chan, ROWS, stride=GROUP), :
        ].astype(bf16)
    own = mixes[pl.ds(chan, ROWS, stride=GROUP), :]
    corr[:, :TAPS] = jnp.dot(own.T.astype(bf16), ahead[...], preferred_element_type=f32)
    acc = corr[0:GROUP, :]
    for group in range(1, LANES // GROUP):
        acc = acc + pltpu.roll(corr[group * GROUP : (group + 1) * GROUP, :], WIDE - group * GROUP, 1)
    for block in range(BLOCKS + 1):
        sums[block, pl.ds(pl.multiple_of(chan * GROUP, GROUP), GROUP), :] = acc[:, block * LANES : (block + 1) * LANES]

    @pl.when(chan == GROUP - 1)
    def _():
        fgrad = None
        for row in range(GROUP):
            part = jnp.concatenate(
                [sums[block, pl.ds(row, GROUP, stride=GROUP), :] for block in range(BLOCKS + 1)], axis=1
            )
            fgrad = part if row == 0 else fgrad + pltpu.roll(part, WIDE - row, 1)
        fgrad_ref[...] = fgrad[:, :TAPS].astype(bf16)


def whole(shape):
    return pl.BlockSpec(shape, lambda chan: (0,) * len(shape))


params = pltpu.CompilerParams(vmem_limit_bytes=48 * 1024 * 1024)
smem = pl.BlockSpec(memory_space=pltpu.SMEM)
taps_spec = pl.BlockSpec((1, TAPS, LANES), lambda chan: (chan, 0, 0))


def early(filters, skip, pair):
    return pl.pallas_call(
        early_kernel,
        grid=(GROUP,),
        in_specs=[whole((GROUP, TAPS)), smem, whole((2 * SIGNAL, LANES))],
        out_specs=[whole((SIGNAL, LANES)), whole((BLOCKS * GROUP, SEQS * LANES)), taps_spec],
        out_shape=[
            jax.ShapeDtypeStruct((SIGNAL, LANES), bf16),
            jax.ShapeDtypeStruct((BLOCKS * GROUP, SEQS * LANES), bf16),
            jax.ShapeDtypeStruct((GROUP, TAPS, LANES), bf16),
        ],
        scratch_shapes=[
            pltpu.VMEM((BLOCKS + 1, GROUP * GROUP, LANES), f32),
            pltpu.VMEM((2 * SIGNAL, LANES), f32),
            pltpu.VMEM((ROWS, TAPS), bf16),
            pltpu.VMEM((LANES, TAPS), bf16),
            pltpu.VMEM((SIGNAL, LANES), f32),
        ],
        compiler_params=params,
        name="early",
    )(filters, skip, pair)


def late_conv(taps, skip, place, pair, value, dmix):
    return pl.pallas_call(
        conv_kernel,
        grid=(GROUP,),
        in_specs=[
            taps_spec,
            smem,
            smem,
            whole((2 * SIGNAL, LANES)),
            whole((BLOCKS * GROUP // 2, 2 * SEQS * LANES)),
            whole((SIGNAL, LANES)),
        ],
        out_specs=[whole((2 * SIGNAL, LANES)), whole((SIGNAL, LANES))],
        out_shape=[
            jax.ShapeDtypeStruct((2 * SIGNAL, LANES), bf16),
            jax.ShapeDtypeStruct((SIGNAL, LANES), bf16),
        ],
        scratch_shapes=[
            pltpu.VMEM((2 * SIGNAL, LANES), f32),
            pltpu.VMEM((SIGNAL, LANES), f32),
            pltpu.VMEM((ROWS, TAPS), bf16),
            pltpu.VMEM((SIGNAL, LANES), f32),
        ],
        compiler_params=params,
        name="late_conv",
    )(taps, skip, place, pair, value, dmix)


def late_fgrad(pair, mix):
    return pl.pallas_call(
        fgrad_kernel,
        grid=(GROUP,),
        in_specs=[whole((2 * SIGNAL, LANES)), whole((SIGNAL, LANES))],
        out_specs=whole((GROUP, TAPS)),
        out_shape=jax.ShapeDtypeStruct((GROUP, TAPS), bf16),
        scratch_shapes=[
            pltpu.VMEM((SIGNAL, LANES), f32),
            pltpu.VMEM((2 * SIGNAL, LANES), f32),
            pltpu.VMEM((ROWS, TAPS), bf16),
            pltpu.VMEM((LANES, WIDE), f32),
            pltpu.VMEM((BLOCKS + 1, GROUP * GROUP, LANES), f32),
        ],
        compiler_params=params,
        name="late_fgrad",
    )(pair, mix)


def swap(values, axes, groups=None):
    return lax.all_to_all(values, axes, split_axis=0, concat_axis=0, tiled=True, axis_index_groups=groups)


def flip(values, axis, bit, extent):
    return lax.ppermute(values, axis, [(i, i ^ bit) for i in range(extent)])


def shift(values, step):
    return lax.ppermute(values, "tensor", [(i, (i + step) % 4) for i in range(4)])


def pick_columns(weight, quarter):
    span = 1024
    source = lax.broadcasted_iota(jnp.int32, (span, 2 * LANES), 0)
    target = lax.broadcasted_iota(jnp.int32, (span, 2 * LANES), 1)
    wanted = (target % LANES // GROUP) * 64 + (target // LANES) * 32 + quarter * GROUP + target % GROUP
    chosen = (source == wanted).astype(bf16)
    parts = [
        jnp.dot(weight[:, start : start + span], chosen, preferred_element_type=f32).astype(bf16)
        for start in range(0, weight.shape[1], span)
    ]
    return jnp.stack([jnp.concatenate([part[:, side * LANES : (side + 1) * LANES] for part in parts], axis=1) for side in (0, 1)])


def per_device(inputs, value_weight, query, key, filters, skip, cotangent):
    quarter = lax.axis_index("dp")
    column = lax.axis_index("tensor")
    side = lax.axis_index("context") % 2
    place = jnp.stack([side, quarter // 2, quarter % 2]).astype(jnp.int32)
    depth = value_weight.shape[0] * BLOCKS
    half = value_weight.shape[1] // 8

    picked = pick_columns(value_weight, quarter)
    weight = swap(
        jnp.broadcast_to(picked[None], (BLOCKS // 2,) + picked.shape).reshape((BLOCKS,) + picked.shape[1:]),
        "context",
    ).reshape(depth, half)

    tokens = jnp.concatenate([inputs[0], flip(inputs[0], "context", 1, BLOCKS)], axis=0)
    tokens_y = flip(tokens, "dp", 2, SEQS)
    tokens = jnp.concatenate([tokens, tokens_y, flip(tokens, "dp", 1, SEQS), flip(tokens_y, "dp", 1, SEQS)], axis=0)

    partial = lax.dot_general(weight, tokens, (((0,), (1,)), ((), ())), preferred_element_type=f32).astype(bf16)
    partial = partial.reshape(4, half // 4, partial.shape[1])

    def block_of(values, index):
        return lax.dynamic_index_in_dim(values, index % 4, 0, keepdims=False)

    received = [shift(block_of(partial, column + step), step) for step in (1, 2, 3)]
    value = block_of(partial, column).astype(f32)
    for part in received:
        value = value + part.astype(f32)
    value = value.astype(bf16)

    query_part = query[0].astype(f32)
    upstream = cotangent[0].astype(f32)
    dconv = (upstream * query_part).astype(bf16)
    pair = jnp.concatenate([dconv.reshape(ROWS, 1, GROUP, LANES), key[0].reshape(ROWS, 1, GROUP, LANES)], axis=1)
    pair, weight_done = lax.optimization_barrier((pair, weight))
    pair = swap(pair, ("context", "dp"))

    value = value.reshape(BLOCKS // 2, GROUP, 2 * SEQS * LANES)
    value, pair = lax.optimization_barrier((value, pair))
    pair = pair.reshape(2 * SIGNAL, LANES)
    groups = [[2 * k + s for k in range(BLOCKS // 2)] for s in (0, 1)]
    value = swap(value, "context", groups)

    own_filters = lax.dynamic_slice_in_dim(filters, quarter * GROUP, GROUP, 0)
    own_skip = lax.dynamic_slice_in_dim(skip, quarter * GROUP, GROUP, 0)
    dmix, dvalue, taps = early(own_filters, own_skip, pair)
    dvalue, value = lax.optimization_barrier((dvalue, value))
    dvalue = swap(dvalue.reshape(BLOCKS, GROUP, SEQS * LANES), "context")

    value = value.reshape(BLOCKS * GROUP // 2, 2 * SEQS * LANES)
    out, mix = late_conv(taps, own_skip, place, pair, value, dmix)
    out, dvalue = lax.optimization_barrier((out, dvalue))
    out = swap(out.reshape(ROWS, 2, GROUP, LANES), ("context", "dp"))
    fgrad = late_fgrad(pair, mix)
    filter_grad = lax.all_gather(fgrad, "dp", axis=0, tiled=True).astype(f32)
    skip_grad = filter_grad[:, 0]

    dvalue = dvalue.reshape(BLOCKS // 2, 2, GROUP, SEQS * LANES)
    sides = [
        lax.dynamic_index_in_dim(dvalue, index, 1, keepdims=False).reshape(LANES, SEQS * LANES)
        for index in (side, 1 - side)
    ]
    dvalue = jnp.concatenate(sides, axis=0)
    dvalue = jnp.concatenate([dvalue] + [shift(dvalue, -step) for step in (1, 2, 3)], axis=0)
    other = flip(weight_done, "context", 1, BLOCKS)
    columns = []
    for step in range(4):
        for part in (weight_done, other):
            columns.append(lax.dynamic_slice_in_dim(part, (column + step) % 4 * LANES, LANES, 1))
    weight_all = jnp.concatenate(columns, axis=1)
    grad = lax.dot_general(dvalue, weight_all, (((0,), (1,)), ((), ())), preferred_element_type=f32).astype(bf16)
    grad = grad.reshape(SEQS, LANES, depth)
    received = [flip(block_of(grad, quarter ^ step), "dp", step, SEQS) for step in (1, 2, 3)]
    input_grad = block_of(grad, quarter).astype(f32)
    for part in received:
        input_grad = input_grad + part.astype(f32)
    input_grad = input_grad.astype(bf16)

    conv = out[:, 0].reshape(SIGNAL, LANES).astype(f32)
    key_grad = out[:, 1].reshape(SIGNAL, LANES)
    gated = (query_part * conv).astype(bf16)
    query_grad = (upstream * conv).astype(bf16)
    return (gated[None], query_grad[None], key_grad[None], input_grad[None], filter_grad, skip_grad)


def solution(mesh):
    by_channel = P("dp", "tensor", "context")
    by_row = P(("tensor", "context"), None)
    in_specs = (
        P("dp", "context", "tensor"),
        by_row,
        by_channel,
        by_channel,
        by_row,
        P(("tensor", "context")),
        by_channel,
    )
    out_specs = (
        by_channel,
        by_channel,
        by_channel,
        P("dp", "context", "tensor"),
        by_row,
        P(("tensor", "context")),
    )
    return jax.shard_map(
        per_device, mesh=mesh, in_specs=in_specs, out_specs=out_specs, check_vma=False
    )
```

```python
import jax
import jax.numpy as jnp
from jax import lax
from jax.experimental import pallas as pl
from jax.experimental.pallas import tpu as pltpu
from jax.sharding import PartitionSpec as P

f32 = jnp.float32
bf16 = jnp.bfloat16

LANES = 128
GROUP = 8
SEQS = 4
BLOCKS = 32
ROWS = BLOCKS * SEQS
SIGNAL = ROWS * GROUP
TAPS = BLOCKS * LANES
WIDE = TAPS + LANES
NEAR = ((0, 0), (1, 0), (3, 0), (2, 0), (2, 1), (3, 1), (1, 1), (0, 1))
HALF = 16
SPAN = 1024


def pack_kernel(quarter_ref, weight_ref, query_ref, upstream_ref, key_ref, out_ref, picks):
    step = pl.program_id(0)

    @pl.when(step == 0)
    def _():
        quarter = quarter_ref[0]
        source = lax.broadcasted_iota(jnp.int32, (SPAN, SPAN), 0)
        target = lax.broadcasted_iota(jnp.int32, (SPAN, SPAN), 1)
        wanted = (target % LANES // 4) * 32 + (target // LANES % SEQS) * GROUP + (target // LANES // SEQS) * 4 + target % 4
        chosen = (source == wanted).astype(f32).astype(bf16)
        row = pl.multiple_of(quarter // 2 * HALF, HALF)
        for slot in range(2):
            lane = pl.multiple_of((quarter % 2 * 2 + slot) * SPAN, SPAN)
            part = weight_ref[pl.ds(row, HALF), pl.ds(lane, SPAN)]
            picked = jnp.dot(part, chosen, preferred_element_type=f32).astype(bf16)
            for kind in range(GROUP):
                start = (kind * 2 + slot) * HALF
                picks[start : start + HALF, :] = picked[:, kind * LANES : (kind + 1) * LANES]

    dconv = upstream_ref[...].astype(f32) * query_ref[...].astype(f32)
    count = dconv.shape[0] // GROUP
    both = [dconv.reshape(count, 1, GROUP, LANES), key_ref[...].astype(f32).reshape(count, 1, GROUP, LANES)]
    both = jnp.concatenate(both, axis=1).reshape(count * HALF, LANES).astype(bf16)
    for dest in range(count):
        kind = dest % GROUP
        out_ref[dest * 48 : dest * 48 + 32, :] = picks[kind * 32 : kind * 32 + 32, :]
        out_ref[dest * 48 + 32 : dest * 48 + 48, :] = both[dest * HALF : (dest + 1) * HALF, :]


def load_pair(pair_ref):
    both = pair_ref[...].astype(f32).reshape(ROWS, 2, GROUP, LANES)
    return both[:, 0].reshape(SIGNAL, LANES), both[:, 1].reshape(SIGNAL, LANES)


def taps_kernel(filters_ref, taps_ref, rolled):
    chan = pl.program_id(0)

    @pl.when(chan == 0)
    def _():
        padded = jnp.concatenate([filters_ref[...], jnp.zeros((GROUP, LANES), f32)], axis=1)
        for row in range(GROUP):
            turned = pltpu.roll(padded, row, 1) if row else padded
            for block in range(BLOCKS + 1):
                rolled[block, row * GROUP : (row + 1) * GROUP, :] = turned[:, block * LANES : (block + 1) * LANES]

    base = jnp.concatenate(
        [rolled[block, pl.ds(chan, GROUP, stride=GROUP), :] for block in range(BLOCKS + 1)], axis=1
    )
    for pair in range(LANES // 16):
        low = pltpu.roll(base, 16 * pair, 1) if pair else base
        high = pltpu.roll(base, 16 * pair + 8, 1)
        tile = jnp.concatenate([low[:, :TAPS], high[:, :TAPS]], axis=0).astype(bf16)
        for block in range(BLOCKS):
            taps_ref[0, block * LANES + 16 * pair : block * LANES + 16 * pair + 16, :] = tile[
                :, block * LANES : (block + 1) * LANES
            ]


def fill_ahead(grads, copies, chan):
    for part in range(SEQS):
        copies[part, 0:ROWS, :] = grads[pl.ds(part * SEQS * GROUP + chan, ROWS, stride=GROUP), :].astype(bf16)


def ahead_of(copies, block):
    return copies[block % 4, block // 4 * 16 : block // 4 * 16 + ROWS, :]


def clear_ahead(grads, copies, dconv):
    grads[0:SIGNAL, :] = dconv
    grads[SIGNAL:, :] = jnp.zeros((LANES, LANES), f32)
    for part in range(SEQS):
        copies[part, ROWS:, :] = jnp.zeros((ROWS, LANES), bf16)


def dmix_kernel(taps0, taps1, taps2, taps3, skip_ref, pair_ref, dmix_ref, dvalue_ref, grads, copies, result):
    chan = pl.program_id(0)

    @pl.when(chan == 0)
    def _():
        clear_ahead(grads, copies, load_pair(pair_ref)[0])

    fill_ahead(grads, copies, chan)
    ahead = jnp.concatenate([ahead_of(copies, block) for block in range(BLOCKS)], axis=1)
    refs = (taps0, taps1, taps2, taps3)
    wide = jnp.concatenate(
        [refs[block // 8][0, block % 8 * LANES : (block % 8 + 1) * LANES, :] for block in range(BLOCKS)], axis=1
    )
    total = lax.dot_general(ahead, wide, (((1,), (1,)), ((), ())), preferred_element_type=f32)
    own = grads[pl.ds(chan, ROWS, stride=GROUP), :]
    result[pl.ds(chan, ROWS, stride=GROUP), :] = total + skip_ref[chan] * own

    @pl.when(chan == GROUP - 1)
    def _():
        _, key = load_pair(pair_ref)
        dmix = result[...].astype(bf16)
        dmix_ref[...] = dmix
        dvalue = (dmix.astype(f32) * key).reshape(BLOCKS, SEQS, GROUP, LANES)
        for seq in range(SEQS):
            dvalue_ref[:, seq * LANES : (seq + 1) * LANES] = (
                dvalue[:, seq].reshape(BLOCKS * GROUP, LANES).astype(bf16)
            )


def project_kernel(column_ref, packed_ref, tokens_ref, out0, out1, out2, out3, low_ref, high_ref):
    part = packed_ref[...].reshape(SPAN, LANES)
    index = (column_ref[0] + pl.program_id(0)) % 4
    lanes = pl.ds(pl.multiple_of(index % 2 * LANES, LANES), LANES)

    @pl.when(index < 2)
    def _():
        low_ref[:, lanes] = part

    @pl.when(index >= 2)
    def _():
        high_ref[:, lanes] = part

    product = lax.dot_general(part, tokens_ref[...], (((0,), (1,)), ((), ())), preferred_element_type=f32)
    product = product.astype(bf16)
    for step, out_ref in enumerate((out0, out1, out2, out3)):

        @pl.when(pl.program_id(0) == step)
        def _():
            out_ref[...] = product


def halves_of(even, odd):
    upper = lax.broadcasted_iota(jnp.int32, even.shape, 0) < 4
    return jnp.where(upper, even, pltpu.roll(odd, 4, 0)), jnp.where(upper, pltpu.roll(even, 4, 0), odd)


def join_kernel(part0, part1, part2, part3, dvalue_ref, out_ref):
    value = part0[...].astype(f32) + part1[...].astype(f32) + part2[...].astype(f32) + part3[...].astype(f32)
    value = value.astype(bf16).astype(f32)
    dvalue = dvalue_ref[...].astype(f32)
    lanes = SEQS * LANES
    for two in range(BLOCKS // 2):
        rows = value[two * GROUP : (two + 1) * GROUP, :]
        for place, tile in enumerate(halves_of(rows[:, :lanes], rows[:, lanes:])):
            index = 2 * two + place
            tile = jnp.concatenate([tile, dvalue[index * GROUP : (index + 1) * GROUP, :]], axis=0)
            out_ref[index * HALF : (index + 1) * HALF, :] = tile.astype(bf16)


def back_kernel(place_ref, dvalue_ref, low, high, other_low, other_high, fgrad_ref, sent_ref, kept_ref, total):
    first = place_ref[0] == 0
    for index in range(4):
        dvalue = dvalue_ref[index * BLOCKS * GROUP : (index + 1) * BLOCKS * GROUP, :].astype(f32)
        tiles = [[], []]
        for two in range(BLOCKS // 2):
            start = two * HALF
            pair = halves_of(dvalue[start : start + GROUP, :], dvalue[start + GROUP : start + HALF, :])
            for half in range(2):
                tiles[half].append(pair[half])
        upper, lower = [jnp.concatenate(part, axis=0).astype(bf16) for part in tiles]
        rows = jnp.concatenate([jnp.where(first, upper, lower), jnp.where(first, lower, upper)], axis=0)
        lanes = slice(index % 2 * LANES, (index % 2 + 1) * LANES)
        columns = [ref[:, lanes] for ref in ((low, other_low) if index < 2 else (high, other_high))]
        columns = jnp.concatenate(columns, axis=1)
        term = lax.dot_general(rows, columns, (((0,), (1,)), ((), ())), preferred_element_type=f32)
        total[...] = term if index == 0 else total[...] + term
    core = place_ref[1]
    for chip in range(2):
        rows = slice(chip * LANES, (chip + 1) * LANES)
        sent_ref[rows, :] = total[pl.ds((2 * chip + 1 - core) * LANES, LANES), :].astype(bf16)
        kept_ref[rows, :] = total[pl.ds((2 * chip + core) * LANES, LANES), :]
    for part in range(4):
        rows = slice(2 * LANES + part * GROUP, 2 * LANES + (part + 1) * GROUP)
        sent_ref[rows, :] = fgrad_ref[:, part * SPAN : (part + 1) * SPAN].astype(bf16)


def middle_kernel(place_ref, kept_ref, received_ref, fgrad_ref, sent_ref, rest_ref):
    chip, core = place_ref[2], place_ref[1]
    for target, index in ((sent_ref, 1 - chip), (rest_ref, chip)):
        rows = pl.ds(pl.multiple_of(index * LANES, LANES), LANES)
        target[0:LANES, :] = (kept_ref[rows, :] + received_ref[rows, :].astype(f32)).astype(bf16)
    own = fgrad_ref[...]
    for part in range(4):
        theirs = received_ref[2 * LANES :, :][part * GROUP : (part + 1) * GROUP, :].astype(f32)
        ours = own[:, part * SPAN : (part + 1) * SPAN]
        both = jnp.concatenate([jnp.where(core == 0, ours, theirs), jnp.where(core == 0, theirs, ours)], axis=0)
        for target in (sent_ref, rest_ref):
            target[LANES + part * HALF : LANES + (part + 1) * HALF, :] = both.astype(bf16)


def last_kernel(place_ref, rest_ref, received_ref, grad_ref, fgrad_ref):
    first = place_ref[2] == 0
    rest, received = rest_ref[...].astype(f32), received_ref[...].astype(f32)
    grad_ref[...] = (rest[0:LANES, :] + received[0:LANES, :]).astype(bf16)
    for part in range(4):
        rows = slice(LANES + part * HALF, LANES + (part + 1) * HALF)
        lanes = slice(part * SPAN, (part + 1) * SPAN)
        fgrad_ref[0:HALF, lanes] = jnp.where(first, rest[rows, :], received[rows, :])
        fgrad_ref[HALF:, lanes] = jnp.where(first, received[rows, :], rest[rows, :])


def conv_kernel(taps0, taps1, taps2, taps3, skip_ref, pair_ref, value_ref, dmix_ref, out_ref, mix_ref, mixes, values, copies, result):
    chan = pl.program_id(0)

    @pl.when(chan == 0)
    def _():
        _, key = load_pair(pair_ref)
        value = value_ref[...].astype(f32)
        for two in range(BLOCKS // 2):
            start = two * 2 * HALF
            pair = halves_of(value[start : start + GROUP, :], value[start + HALF : start + HALF + GROUP, :])
            for side in range(2):
                for piece, (seq, _) in enumerate(NEAR[side * SEQS : (side + 1) * SEQS]):
                    row = ((2 * two + side) * SEQS + seq) * GROUP
                    values[row : row + GROUP, :] = pair[side][:, piece * LANES : (piece + 1) * LANES]
        mix = (key * values[...]).astype(bf16)
        mix_ref[...] = mix
        mixes[0:LANES, :] = jnp.zeros((LANES, LANES), f32)
        mixes[LANES:, :] = mix.astype(f32)
        for part in range(SEQS):
            copies[part, 0:ROWS, :] = jnp.zeros((ROWS, LANES), bf16)

    for part in range(SEQS):
        copies[part, ROWS:, :] = mixes[
            pl.ds(LANES - part * SEQS * GROUP + chan, ROWS, stride=GROUP), :
        ].astype(bf16)
    behind = [
        copies[block % 4, ROWS - block // 4 * 16 : 2 * ROWS - block // 4 * 16, :] for block in range(BLOCKS)
    ]
    own = mixes[pl.ds(LANES + chan, ROWS, stride=GROUP), :]
    taps = jnp.concatenate([ref[0] for ref in (taps0, taps1, taps2, taps3)], axis=0)
    total = jnp.dot(jnp.concatenate(behind, axis=1), taps, preferred_element_type=f32)
    result[pl.ds(chan, ROWS, stride=GROUP), :] = total + skip_ref[chan] * own

    @pl.when(chan == GROUP - 1)
    def _():
        kgrad = dmix_ref[...].astype(f32) * values[...]
        both = [result[...].reshape(ROWS, 1, GROUP, LANES), kgrad.reshape(ROWS, 1, GROUP, LANES)]
        out_ref[...] = jnp.concatenate(both, axis=1).reshape(2 * SIGNAL, LANES).astype(bf16)


def fgrad_kernel(pair_ref, mix_ref, fgrad_ref, mixes, grads, copies, corr, sums):
    chan = pl.program_id(0)

    @pl.when(chan == 0)
    def _():
        clear_ahead(grads, copies, load_pair(pair_ref)[0])
        mixes[...] = mix_ref[...].astype(f32)
        corr[:, TAPS:] = jnp.zeros((LANES, LANES), f32)

    fill_ahead(grads, copies, chan)
    own = mixes[pl.ds(chan, ROWS, stride=GROUP), :].T.astype(bf16)
    for block in range(0, BLOCKS, 2):
        two = jnp.concatenate([ahead_of(copies, block), ahead_of(copies, block + 1)], axis=1)
        corr[:, block * LANES : (block + 2) * LANES] = jnp.dot(own, two, preferred_element_type=f32)
    acc = corr[0:GROUP, :]
    for group in range(1, LANES // GROUP):
        acc = acc + pltpu.roll(corr[group * GROUP : (group + 1) * GROUP, :], WIDE - group * GROUP, 1)
    for block in range(BLOCKS + 1):
        sums[block, pl.ds(pl.multiple_of(chan * GROUP, GROUP), GROUP), :] = acc[:, block * LANES : (block + 1) * LANES]

    @pl.when(chan == GROUP - 1)
    def _():
        fgrad = None
        for row in range(GROUP):
            part = jnp.concatenate(
                [sums[block, pl.ds(row, GROUP, stride=GROUP), :] for block in range(BLOCKS + 1)], axis=1
            )
            fgrad = part if row == 0 else fgrad + pltpu.roll(part, WIDE - row, 1)
        fgrad_ref[...] = fgrad[:, :TAPS]


def whole(shape):
    return pl.BlockSpec(shape, lambda chan: (0,) * len(shape))


params = pltpu.CompilerParams(vmem_limit_bytes=24 * 1024 * 1024)
smem = pl.BlockSpec(memory_space=pltpu.SMEM)
taps_spec = pl.BlockSpec((1, TAPS, LANES), lambda chan: (chan, 0, 0))
CUTS = 4
CUT = TAPS // CUTS
taps_specs = [pl.BlockSpec((1, CUT, LANES), lambda chan, cut=cut: (chan, cut, 0)) for cut in range(CUTS)]
pair_spec = pl.BlockSpec((ROWS, 1, HALF, LANES), lambda chan: (0, 2, 0, 0))


def pack(quarter, weight, query, upstream, key):
    steps = 4
    block = pl.BlockSpec((SIGNAL // steps, LANES), lambda step: (step, 0))
    return pl.pallas_call(
        pack_kernel,
        grid=(steps,),
        in_specs=[smem, pl.BlockSpec(weight.shape, lambda step: (0, 0)), block, block, block],
        out_specs=pl.BlockSpec((ROWS * 48 // steps, LANES), lambda step: (step, 0)),
        out_shape=jax.ShapeDtypeStruct((ROWS * 48, LANES), bf16),
        scratch_shapes=[pltpu.VMEM((2 * GROUP * HALF, LANES), bf16)],
        compiler_params=params,
        name="pack",
    )(quarter, *[pltpu.with_memory_space_constraint(x, pltpu.HBM) for x in (weight, query, upstream, key)])


def build_taps(filters):
    return pl.pallas_call(
        taps_kernel,
        grid=(GROUP,),
        in_specs=[whole((GROUP, TAPS))],
        out_specs=taps_spec,
        out_shape=jax.ShapeDtypeStruct((GROUP, TAPS, LANES), bf16),
        scratch_shapes=[pltpu.VMEM((BLOCKS + 1, GROUP * GROUP, LANES), f32)],
        compiler_params=params,
        name="build_taps",
    )(filters)


def early_dmix(taps, skip, pair):
    return pl.pallas_call(
        dmix_kernel,
        grid=(GROUP,),
        in_specs=taps_specs + [smem, pair_spec],
        out_specs=[whole((SIGNAL, LANES)), whole((BLOCKS * GROUP, SEQS * LANES))],
        out_shape=[
            jax.ShapeDtypeStruct((SIGNAL, LANES), bf16),
            jax.ShapeDtypeStruct((BLOCKS * GROUP, SEQS * LANES), bf16),
        ],
        scratch_shapes=[
            pltpu.VMEM((SIGNAL + LANES, LANES), f32),
            pltpu.VMEM((SEQS, 2 * ROWS, LANES), bf16),
            pltpu.VMEM((SIGNAL, LANES), f32),
        ],
        compiler_params=params,
        name="early_dmix",
    )(taps, taps, taps, taps, skip, pair)


def project(column, packed, tokens):
    slots = packed.reshape(2 * BLOCKS, 2, 3, HALF, LANES)

    def slot(step, column_ref):
        part = (column_ref[0] + step) % 4
        return (0, part // 2, part % 2, 0, 0)

    out_spec = pl.BlockSpec((LANES, tokens.shape[0]), lambda step, column_ref: (0, 0))
    return pl.pallas_call(
        project_kernel,
        grid_spec=pltpu.PrefetchScalarGridSpec(
            num_scalar_prefetch=1,
            grid=(4,),
            in_specs=[
                pl.BlockSpec((2 * BLOCKS, 1, 1, HALF, LANES), slot),
                pl.BlockSpec(tokens.shape, lambda step, column_ref: (0, 0)),
            ],
            out_specs=[out_spec] * 4 + [pl.BlockSpec((SPAN, 2 * LANES), lambda step, column_ref: (0, 0))] * 2,
        ),
        out_shape=[jax.ShapeDtypeStruct((LANES, tokens.shape[0]), bf16)] * 4
        + [jax.ShapeDtypeStruct((SPAN, 2 * LANES), bf16)] * 2,
        compiler_params=params,
        name="project",
    )(column, slots, tokens)


def join(parts, dvalue):
    return pl.pallas_call(
        join_kernel,
        out_shape=jax.ShapeDtypeStruct((BLOCKS * HALF, SEQS * LANES), bf16),
        compiler_params=params,
        name="join",
    )(*parts, dvalue)


def vmem_specs(count):
    return [smem] + [pl.BlockSpec(memory_space=pltpu.VMEM)] * count


def back(place, dvalue, weights, fgrad):
    return pl.pallas_call(
        back_kernel,
        in_specs=vmem_specs(6),
        out_shape=[
            jax.ShapeDtypeStruct((2 * LANES + 4 * GROUP, SPAN), bf16),
            jax.ShapeDtypeStruct((2 * LANES, SPAN), f32),
        ],
        scratch_shapes=[pltpu.VMEM((SEQS * LANES, SPAN), f32)],
        compiler_params=params,
        name="back",
    )(place, dvalue, *weights, fgrad)


def middle(place, kept, received, fgrad):
    return pl.pallas_call(
        middle_kernel,
        in_specs=vmem_specs(3),
        out_shape=[jax.ShapeDtypeStruct((LANES + 4 * HALF, SPAN), bf16)] * 2,
        compiler_params=params,
        name="middle",
    )(place, kept, received, fgrad)


def last(place, rest, received):
    return pl.pallas_call(
        last_kernel,
        in_specs=vmem_specs(2),
        out_shape=[jax.ShapeDtypeStruct((LANES, SPAN), bf16), jax.ShapeDtypeStruct((2 * HALF, TAPS), f32)],
        compiler_params=params,
        name="last",
    )(place, rest, received)


def late_conv(taps, skip, pair, value, dmix):
    return pl.pallas_call(
        conv_kernel,
        grid=(GROUP,),
        in_specs=taps_specs
        + [
            smem,
            pair_spec,
            whole((BLOCKS * HALF, SEQS * LANES)),
            whole((SIGNAL, LANES)),
        ],
        out_specs=[whole((2 * SIGNAL, LANES)), whole((SIGNAL, LANES))],
        out_shape=[
            jax.ShapeDtypeStruct((2 * SIGNAL, LANES), bf16),
            jax.ShapeDtypeStruct((SIGNAL, LANES), bf16),
        ],
        scratch_shapes=[
            pltpu.VMEM((SIGNAL + LANES, LANES), f32),
            pltpu.VMEM((SIGNAL, LANES), f32),
            pltpu.VMEM((SEQS, 2 * ROWS, LANES), bf16),
            pltpu.VMEM((SIGNAL, LANES), f32),
        ],
        compiler_params=params,
        name="late_conv",
    )(taps, taps, taps, taps, skip, pair, value, dmix)


def late_fgrad(pair, mix):
    return pl.pallas_call(
        fgrad_kernel,
        grid=(GROUP,),
        in_specs=[pair_spec, whole((SIGNAL, LANES))],
        out_specs=whole((GROUP, TAPS)),
        out_shape=jax.ShapeDtypeStruct((GROUP, TAPS), f32),
        scratch_shapes=[
            pltpu.VMEM((SIGNAL, LANES), f32),
            pltpu.VMEM((SIGNAL + LANES, LANES), f32),
            pltpu.VMEM((SEQS, 2 * ROWS, LANES), bf16),
            pltpu.VMEM((LANES, WIDE), f32),
            pltpu.VMEM((BLOCKS + 1, GROUP * GROUP, LANES), f32),
        ],
        compiler_params=params,
        name="late_fgrad",
    )(pair, mix)


def swap(values, axes, groups=None):
    return lax.all_to_all(values, axes, split_axis=0, concat_axis=0, tiled=True, axis_index_groups=groups)


def per_device(inputs, value_weight, query, key, filters, skip, cotangent):
    quarter = lax.axis_index("dp")
    side = lax.axis_index("context") % 2

    near = [[seq * BLOCKS + 2 * k + place for seq, place in NEAR] for k in range(BLOCKS // 2)]
    tokens = lax.all_gather(inputs[0], ("dp", "context"), axis=0, tiled=True, axis_index_groups=near)
    own_filters = lax.dynamic_slice_in_dim(filters, quarter * GROUP, GROUP, 0)
    own_skip = lax.dynamic_slice_in_dim(skip, quarter * GROUP, GROUP, 0)
    taps = build_taps(own_filters)

    packed = pack(quarter.astype(jnp.int32)[None], value_weight, query[0], cotangent[0], key[0])
    packed = swap(packed.reshape(ROWS, 3 * HALF, LANES), ("context", "dp"))
    packed, taps = lax.optimization_barrier((packed, taps))
    pair = packed.reshape(ROWS, 3, HALF, LANES)

    column = lax.axis_index("tensor").astype(jnp.int32)[None]
    *parts, low, high = project(column, packed, tokens)
    parts = [parts[0]] + [
        lax.ppermute(parts[step], "tensor", [(i, (i + step) % 4) for i in range(4)]) for step in (1, 2, 3)
    ]
    twins = [(k, k ^ 1) for k in range(BLOCKS)]
    other_low = lax.ppermute(low, "context", twins)
    dmix, dvalue = early_dmix(taps, own_skip, pair)
    dvalue, other_low = lax.optimization_barrier((dvalue, other_low))

    both, high = lax.optimization_barrier((join(parts, dvalue), high))
    other_high = lax.ppermute(high, "context", twins)
    both = swap(both.reshape(BLOCKS, HALF, SEQS * LANES), "context")
    dvalue = lax.all_gather(both[:, GROUP:].reshape(BLOCKS * GROUP, SEQS * LANES), "tensor", axis=0, tiled=True)
    out, mix = late_conv(taps, own_skip, pair, both.reshape(BLOCKS * HALF, SEQS * LANES), dmix)
    out = swap(out.reshape(ROWS, 2, GROUP, LANES), ("context", "dp"))
    fgrad = late_fgrad(pair, mix)
    dvalue, fgrad = lax.optimization_barrier((dvalue, fgrad))

    place = jnp.stack([side, quarter % 2, quarter // 2]).astype(jnp.int32)
    sent, kept = back(place, dvalue, (low, high, other_low, other_high), fgrad)
    received = lax.ppermute(sent, "dp", [(i, i ^ 1) for i in range(SEQS)])
    sent, rest = middle(place, kept, received, fgrad)
    received = lax.ppermute(sent, "dp", [(i, i ^ 2) for i in range(SEQS)])
    input_grad, filter_grad = last(place, rest, received)
    skip_grad = filter_grad[:, 0]

    query_part = query[0].astype(f32)
    upstream = cotangent[0].astype(f32)
    conv = out[:, 0].reshape(SIGNAL, LANES).astype(f32)
    key_grad = out[:, 1].reshape(SIGNAL, LANES)
    gated = (query_part * conv).astype(bf16)
    query_grad = (upstream * conv).astype(bf16)
    return (gated[None], query_grad[None], key_grad[None], input_grad[None], filter_grad, skip_grad)


def solution(mesh):
    by_channel = P("dp", "tensor", "context")
    by_row = P(("tensor", "context"), None)
    in_specs = (
        P("dp", "context", "tensor"),
        by_row,
        by_channel,
        by_channel,
        by_row,
        P(("tensor", "context")),
        by_channel,
    )
    out_specs = (
        by_channel,
        by_channel,
        by_channel,
        P("dp", "context", "tensor"),
        by_row,
        P(("tensor", "context")),
    )
    return jax.shard_map(
        per_device, mesh=mesh, in_specs=in_specs, out_specs=out_specs, check_vma=False
    )
```

```python
import jax
import jax.numpy as jnp
from jax import lax
from jax.experimental import pallas as pl
from jax.experimental.pallas import tpu as pltpu
from jax.sharding import PartitionSpec as P

f32 = jnp.float32
bf16 = jnp.bfloat16

LANES = 128
GROUP = 8
SEQS = 4
BLOCKS = 32
ROWS = BLOCKS * SEQS
SIGNAL = ROWS * GROUP
TAPS = BLOCKS * LANES
WIDE = TAPS + LANES
NEAR = ((0, 0), (1, 0), (3, 0), (2, 0), (2, 1), (3, 1), (1, 1), (0, 1))
HALF = 16
SPAN = 1024


def pack_kernel(quarter_ref, weight_ref, out_ref, picks):
    @pl.when(pl.program_id(0) == 0)
    def _():
        source = lax.broadcasted_iota(jnp.int32, (SPAN, 2 * LANES), 0)
        target = lax.broadcasted_iota(jnp.int32, (SPAN, 2 * LANES), 1)
        wanted = (target % LANES // 4) * 32 + quarter_ref[0] * GROUP + (target // LANES) * 4 + target % 4
        chosen = (source == wanted).astype(f32).astype(bf16)
        for part in range(4):
            columns = weight_ref[:, part * SPAN : (part + 1) * SPAN]
            picked = jnp.dot(columns, chosen, preferred_element_type=f32).astype(bf16)
            for side in range(2):
                picks[side, :, part * LANES : (part + 1) * LANES] = picked[:, side * LANES : (side + 1) * LANES]

    count = picks.shape[1]
    for dest in range(out_ref.shape[0] // count):
        out_ref[dest * count : (dest + 1) * count, :] = picks[dest % 2]


def load_pair(pair_ref):
    both = pair_ref[...].astype(f32).reshape(ROWS, 2, GROUP, LANES)
    return both[:, 0].reshape(SIGNAL, LANES), both[:, 1].reshape(SIGNAL, LANES)


def taps_kernel(filters_ref, taps_ref, rolled):
    chan = pl.program_id(0)

    @pl.when(chan == 0)
    def _():
        padded = jnp.concatenate([filters_ref[...], jnp.zeros((GROUP, LANES), f32)], axis=1)
        for row in range(GROUP):
            turned = pltpu.roll(padded, row, 1) if row else padded
            for block in range(BLOCKS + 1):
                rolled[block, row * GROUP : (row + 1) * GROUP, :] = turned[:, block * LANES : (block + 1) * LANES]

    base = jnp.concatenate(
        [rolled[block, pl.ds(chan, GROUP, stride=GROUP), :] for block in range(BLOCKS + 1)], axis=1
    )
    for pair in range(LANES // 16):
        low = pltpu.roll(base, 16 * pair, 1) if pair else base
        high = pltpu.roll(base, 16 * pair + 8, 1)
        tile = jnp.concatenate([low[:, :TAPS], high[:, :TAPS]], axis=0).astype(bf16)
        for block in range(BLOCKS):
            taps_ref[0, block * LANES + 16 * pair : block * LANES + 16 * pair + 16, :] = tile[
                :, block * LANES : (block + 1) * LANES
            ]


def fill_ahead(grads, copies, chan):
    for part in range(SEQS):
        copies[part, 0:ROWS, :] = grads[pl.ds(part * SEQS * GROUP + chan, ROWS, stride=GROUP), :].astype(bf16)


def ahead_of(copies, block):
    return copies[block % 4, block // 4 * 16 : block // 4 * 16 + ROWS, :]


def clear_ahead(grads, copies, dconv):
    grads[0:SIGNAL, :] = dconv
    grads[SIGNAL:, :] = jnp.zeros((LANES, LANES), f32)
    for part in range(SEQS):
        copies[part, ROWS:, :] = jnp.zeros((ROWS, LANES), bf16)


def start_taps(taps_ref, taps, done):
    for chan in range(GROUP):
        pltpu.make_async_copy(taps_ref.at[chan], taps.at[chan], done.at[chan]).start()


def wait_taps(taps_ref, taps, done, chan):
    pltpu.make_async_copy(taps_ref.at[chan], taps.at[chan], done.at[chan]).wait()


def dmix_kernel(taps_ref, skip_ref, pair_ref, dmix_ref, dvalue_ref, taps, done, grads, copies, result):
    chan = pl.program_id(0)

    @pl.when(chan == 0)
    def _():
        start_taps(taps_ref, taps, done)
        clear_ahead(grads, copies, load_pair(pair_ref)[0])

    fill_ahead(grads, copies, chan)
    ahead = jnp.concatenate([ahead_of(copies, block) for block in range(BLOCKS)], axis=1)
    wait_taps(taps_ref, taps, done, chan)
    wide = jnp.concatenate([taps[chan, block * LANES : (block + 1) * LANES, :] for block in range(BLOCKS)], axis=1)
    total = lax.dot_general(ahead, wide, (((1,), (1,)), ((), ())), preferred_element_type=f32)
    own = grads[pl.ds(chan, ROWS, stride=GROUP), :]
    result[pl.ds(chan, ROWS, stride=GROUP), :] = total + skip_ref[chan] * own

    @pl.when(chan == GROUP - 1)
    def _():
        _, key = load_pair(pair_ref)
        dmix = result[...].astype(bf16)
        dmix_ref[...] = dmix
        dvalue = (dmix.astype(f32) * key).reshape(BLOCKS, SEQS, GROUP, LANES)
        for seq in range(SEQS):
            dvalue_ref[:, seq * LANES : (seq + 1) * LANES] = (
                dvalue[:, seq].reshape(BLOCKS * GROUP, LANES).astype(bf16)
            )


def project_kernel(column_ref, weight_ref, tokens_ref, out0, out1, out2, out3, low_ref, high_ref):
    part = weight_ref[...]
    index = (column_ref[0] + pl.program_id(0)) % 4
    lanes = pl.ds(pl.multiple_of(index % 2 * LANES, LANES), LANES)

    @pl.when(index < 2)
    def _():
        low_ref[:, lanes] = part

    @pl.when(index >= 2)
    def _():
        high_ref[:, lanes] = part

    product = lax.dot_general(part, tokens_ref[...], (((0,), (1,)), ((), ())), preferred_element_type=f32)
    product = product.astype(bf16)
    for step, out_ref in enumerate((out0, out1, out2, out3)):

        @pl.when(pl.program_id(0) == step)
        def _():
            out_ref[...] = product


def halves_of(even, odd):
    upper = lax.broadcasted_iota(jnp.int32, even.shape, 0) < 4
    return jnp.where(upper, even, pltpu.roll(odd, 4, 0)), jnp.where(upper, pltpu.roll(even, 4, 0), odd)


def join_kernel(part0, part1, part2, part3, dvalue_ref, out_ref):
    value = part0[...].astype(f32) + part1[...].astype(f32) + part2[...].astype(f32) + part3[...].astype(f32)
    value = value.astype(bf16).astype(f32)
    dvalue = dvalue_ref[...].astype(f32)
    sides = []
    for side in range(2):
        order = [NEAR.index((seq, side)) for seq in range(SEQS)]
        sides.append(jnp.concatenate([value[:, piece * LANES : (piece + 1) * LANES] for piece in order], axis=1))
    for two in range(BLOCKS // 2):
        rows = [part[two * GROUP : (two + 1) * GROUP, :] for part in sides]
        for place, tile in enumerate(halves_of(*rows)):
            index = 2 * two + place
            tile = jnp.concatenate([tile, dvalue[index * GROUP : (index + 1) * GROUP, :]], axis=0)
            out_ref[index * HALF : (index + 1) * HALF, :] = tile.astype(bf16)


def back_kernel(place_ref, dvalue_ref, low, high, other_low, other_high, fgrad_ref, sent_ref, kept_ref, total):
    first = place_ref[0] == 0
    for index in range(4):
        dvalue = dvalue_ref[index * BLOCKS * GROUP : (index + 1) * BLOCKS * GROUP, :].astype(f32)
        tiles = [[], []]
        for two in range(BLOCKS // 2):
            start = two * HALF
            pair = halves_of(dvalue[start : start + GROUP, :], dvalue[start + GROUP : start + HALF, :])
            for half in range(2):
                tiles[half].append(pair[half])
        upper, lower = [jnp.concatenate(part, axis=0).astype(bf16) for part in tiles]
        rows = jnp.concatenate([jnp.where(first, upper, lower), jnp.where(first, lower, upper)], axis=0)
        lanes = slice(index % 2 * LANES, (index % 2 + 1) * LANES)
        columns = [ref[:, lanes] for ref in ((low, other_low) if index < 2 else (high, other_high))]
        columns = jnp.concatenate(columns, axis=1)
        term = lax.dot_general(rows, columns, (((0,), (1,)), ((), ())), preferred_element_type=f32)
        total[...] = term if index == 0 else total[...] + term
    core = place_ref[1]
    for chip in range(2):
        rows = slice(chip * LANES, (chip + 1) * LANES)
        sent_ref[rows, :] = total[pl.ds((2 * chip + 1 - core) * LANES, LANES), :].astype(bf16)
        kept_ref[rows, :] = total[pl.ds((2 * chip + core) * LANES, LANES), :]
    for part in range(4):
        rows = slice(2 * LANES + part * GROUP, 2 * LANES + (part + 1) * GROUP)
        sent_ref[rows, :] = fgrad_ref[:, part * SPAN : (part + 1) * SPAN].astype(bf16)


def middle_kernel(place_ref, kept_ref, received_ref, fgrad_ref, sent_ref, rest_ref):
    chip, core = place_ref[2], place_ref[1]
    for target, index in ((sent_ref, 1 - chip), (rest_ref, chip)):
        rows = pl.ds(pl.multiple_of(index * LANES, LANES), LANES)
        target[0:LANES, :] = (kept_ref[rows, :] + received_ref[rows, :].astype(f32)).astype(bf16)
    own = fgrad_ref[...]
    for part in range(4):
        theirs = received_ref[2 * LANES :, :][part * GROUP : (part + 1) * GROUP, :].astype(f32)
        ours = own[:, part * SPAN : (part + 1) * SPAN]
        both = jnp.concatenate([jnp.where(core == 0, ours, theirs), jnp.where(core == 0, theirs, ours)], axis=0)
        for target in (sent_ref, rest_ref):
            target[LANES + part * HALF : LANES + (part + 1) * HALF, :] = both.astype(bf16)


def last_kernel(place_ref, rest_ref, received_ref, grad_ref, fgrad_ref):
    first = place_ref[2] == 0
    rest, received = rest_ref[...].astype(f32), received_ref[...].astype(f32)
    grad_ref[...] = (rest[0:LANES, :] + received[0:LANES, :]).astype(bf16)
    for part in range(4):
        rows = slice(LANES + part * HALF, LANES + (part + 1) * HALF)
        lanes = slice(part * SPAN, (part + 1) * SPAN)
        fgrad_ref[0:HALF, lanes] = jnp.where(first, rest[rows, :], received[rows, :])
        fgrad_ref[HALF:, lanes] = jnp.where(first, received[rows, :], rest[rows, :])


def conv_kernel(taps_ref, skip_ref, pair_ref, value_ref, dmix_ref, out_ref, mix_ref, taps, done, mixes, values, copies, result):
    chan = pl.program_id(0)

    @pl.when(chan == 0)
    def _():
        start_taps(taps_ref, taps, done)
        _, key = load_pair(pair_ref)
        value = value_ref[...].astype(f32)
        for two in range(BLOCKS // 2):
            start = two * 2 * HALF
            pair = halves_of(value[start : start + GROUP, :], value[start + HALF : start + HALF + GROUP, :])
            for side in range(2):
                for seq in range(SEQS):
                    row = ((2 * two + side) * SEQS + seq) * GROUP
                    values[row : row + GROUP, :] = pair[side][:, seq * LANES : (seq + 1) * LANES]
        mix = (key * values[...]).astype(bf16)
        mix_ref[...] = mix
        mixes[0:LANES, :] = jnp.zeros((LANES, LANES), f32)
        mixes[LANES:, :] = mix.astype(f32)
        for part in range(SEQS):
            copies[part, 0:ROWS, :] = jnp.zeros((ROWS, LANES), bf16)

    for part in range(SEQS):
        copies[part, ROWS:, :] = mixes[
            pl.ds(LANES - part * SEQS * GROUP + chan, ROWS, stride=GROUP), :
        ].astype(bf16)
    behind = [
        copies[block % 4, ROWS - block // 4 * 16 : 2 * ROWS - block // 4 * 16, :] for block in range(BLOCKS)
    ]
    own = mixes[pl.ds(LANES + chan, ROWS, stride=GROUP), :]
    wait_taps(taps_ref, taps, done, chan)
    total = jnp.dot(jnp.concatenate(behind, axis=1), taps[chan], preferred_element_type=f32)
    result[pl.ds(chan, ROWS, stride=GROUP), :] = total + skip_ref[chan] * own

    @pl.when(chan == GROUP - 1)
    def _():
        kgrad = dmix_ref[...].astype(f32) * values[...]
        both = [result[...].reshape(ROWS, 1, GROUP, LANES), kgrad.reshape(ROWS, 1, GROUP, LANES)]
        out_ref[...] = jnp.concatenate(both, axis=1).reshape(2 * SIGNAL, LANES).astype(bf16)


def fgrad_kernel(pair_ref, mix_ref, fgrad_ref, mixes, grads, copies, corr, sums):
    chan = pl.program_id(0)

    @pl.when(chan == 0)
    def _():
        clear_ahead(grads, copies, load_pair(pair_ref)[0])
        mixes[...] = mix_ref[...].astype(f32)
        corr[:, TAPS:] = jnp.zeros((LANES, LANES), f32)

    fill_ahead(grads, copies, chan)
    own = mixes[pl.ds(chan, ROWS, stride=GROUP), :].T.astype(bf16)
    for block in range(0, BLOCKS, 2):
        two = jnp.concatenate([ahead_of(copies, block), ahead_of(copies, block + 1)], axis=1)
        corr[:, block * LANES : (block + 2) * LANES] = jnp.dot(own, two, preferred_element_type=f32)
    acc = corr[0:GROUP, :]
    for group in range(1, LANES // GROUP):
        acc = acc + pltpu.roll(corr[group * GROUP : (group + 1) * GROUP, :], WIDE - group * GROUP, 1)
    for block in range(BLOCKS + 1):
        sums[block, pl.ds(pl.multiple_of(chan * GROUP, GROUP), GROUP), :] = acc[:, block * LANES : (block + 1) * LANES]

    @pl.when(chan == GROUP - 1)
    def _():
        fgrad = None
        for row in range(GROUP):
            part = jnp.concatenate(
                [sums[block, pl.ds(row, GROUP, stride=GROUP), :] for block in range(BLOCKS + 1)], axis=1
            )
            fgrad = part if row == 0 else fgrad + pltpu.roll(part, WIDE - row, 1)
        fgrad_ref[...] = fgrad[:, :TAPS]


def whole(shape):
    return pl.BlockSpec(shape, lambda chan: (0,) * len(shape))


params = pltpu.CompilerParams(vmem_limit_bytes=24 * 1024 * 1024)
smem = pl.BlockSpec(memory_space=pltpu.SMEM)
taps_spec = pl.BlockSpec((1, TAPS, LANES), lambda chan: (chan, 0, 0))
any_spec = pl.BlockSpec(memory_space=pl.ANY)
taps_scratch = [pltpu.VMEM((GROUP, TAPS, LANES), bf16), pltpu.SemaphoreType.DMA((GROUP,))]
pair_spec = whole((2 * SIGNAL, LANES))


def pack(quarter, weight):
    steps, rows = 4, weight.shape[0]
    return pl.pallas_call(
        pack_kernel,
        grid=(steps,),
        in_specs=[smem, pl.BlockSpec(weight.shape, lambda step: (0, 0))],
        out_specs=pl.BlockSpec((rows * BLOCKS // steps, 4 * LANES), lambda step: (step, 0)),
        out_shape=jax.ShapeDtypeStruct((rows * BLOCKS, 4 * LANES), bf16),
        scratch_shapes=[pltpu.VMEM((2, rows, 4 * LANES), bf16)],
        compiler_params=params,
        name="pack",
    )(quarter, pltpu.with_memory_space_constraint(weight, pltpu.HBM))


def build_taps(filters):
    return pl.pallas_call(
        taps_kernel,
        grid=(GROUP,),
        in_specs=[whole((GROUP, TAPS))],
        out_specs=taps_spec,
        out_shape=jax.ShapeDtypeStruct((GROUP, TAPS, LANES), bf16),
        scratch_shapes=[pltpu.VMEM((BLOCKS + 1, GROUP * GROUP, LANES), f32)],
        compiler_params=params,
        name="build_taps",
    )(filters)


def early_dmix(taps, skip, pair):
    return pl.pallas_call(
        dmix_kernel,
        grid=(GROUP,),
        in_specs=[any_spec, smem, pair_spec],
        out_specs=[whole((SIGNAL, LANES)), whole((BLOCKS * GROUP, SEQS * LANES))],
        out_shape=[
            jax.ShapeDtypeStruct((SIGNAL, LANES), bf16),
            jax.ShapeDtypeStruct((BLOCKS * GROUP, SEQS * LANES), bf16),
        ],
        scratch_shapes=taps_scratch
        + [
            pltpu.VMEM((SIGNAL + LANES, LANES), f32),
            pltpu.VMEM((SEQS, 2 * ROWS, LANES), bf16),
            pltpu.VMEM((SIGNAL, LANES), f32),
        ],
        compiler_params=params,
        name="early_dmix",
    )(pltpu.with_memory_space_constraint(taps, pltpu.HBM), skip, pair)


def project(column, weight, tokens):
    count = tokens.shape[0]
    out_spec = pl.BlockSpec((LANES, count), lambda step, column_ref: (0, 0))
    return pl.pallas_call(
        project_kernel,
        grid_spec=pltpu.PrefetchScalarGridSpec(
            num_scalar_prefetch=1,
            grid=(4,),
            in_specs=[
                pl.BlockSpec((SPAN, LANES), lambda step, column_ref: (0, (column_ref[0] + step) % 4)),
                pl.BlockSpec(tokens.shape, lambda step, column_ref: (0, 0)),
            ],
            out_specs=[out_spec] * 4 + [pl.BlockSpec((SPAN, 2 * LANES), lambda step, column_ref: (0, 0))] * 2,
        ),
        out_shape=[jax.ShapeDtypeStruct((LANES, count), bf16)] * 4
        + [jax.ShapeDtypeStruct((SPAN, 2 * LANES), bf16)] * 2,
        compiler_params=params,
        name="project",
    )(column, weight, tokens)


def vmem_specs(count):
    return [smem] + [pl.BlockSpec(memory_space=pltpu.VMEM)] * count


def join(parts, dvalue):
    return pl.pallas_call(
        join_kernel,
        out_shape=jax.ShapeDtypeStruct((BLOCKS * HALF, SEQS * LANES), bf16),
        compiler_params=params,
        name="join",
    )(*parts, dvalue)


def back(place, dvalue, weights, fgrad):
    return pl.pallas_call(
        back_kernel,
        in_specs=vmem_specs(6),
        out_shape=[
            jax.ShapeDtypeStruct((2 * LANES + 4 * GROUP, SPAN), bf16),
            jax.ShapeDtypeStruct((2 * LANES, SPAN), f32),
        ],
        scratch_shapes=[pltpu.VMEM((SEQS * LANES, SPAN), f32)],
        compiler_params=params,
        name="back",
    )(place, dvalue, *weights, fgrad)


def middle(place, kept, received, fgrad):
    return pl.pallas_call(
        middle_kernel,
        in_specs=vmem_specs(3),
        out_shape=[jax.ShapeDtypeStruct((LANES + 4 * HALF, SPAN), bf16)] * 2,
        compiler_params=params,
        name="middle",
    )(place, kept, received, fgrad)


def last(place, rest, received):
    return pl.pallas_call(
        last_kernel,
        in_specs=vmem_specs(2),
        out_shape=[jax.ShapeDtypeStruct((LANES, SPAN), bf16), jax.ShapeDtypeStruct((2 * HALF, TAPS), f32)],
        compiler_params=params,
        name="last",
    )(place, rest, received)


def late_conv(taps, skip, pair, value, dmix):
    return pl.pallas_call(
        conv_kernel,
        grid=(GROUP,),
        in_specs=[
            any_spec,
            smem,
            pair_spec,
            whole((BLOCKS * HALF, SEQS * LANES)),
            whole((SIGNAL, LANES)),
        ],
        out_specs=[whole((2 * SIGNAL, LANES)), whole((SIGNAL, LANES))],
        out_shape=[
            jax.ShapeDtypeStruct((2 * SIGNAL, LANES), bf16),
            jax.ShapeDtypeStruct((SIGNAL, LANES), bf16),
        ],
        scratch_shapes=taps_scratch
        + [
            pltpu.VMEM((SIGNAL + LANES, LANES), f32),
            pltpu.VMEM((SIGNAL, LANES), f32),
            pltpu.VMEM((SEQS, 2 * ROWS, LANES), bf16),
            pltpu.VMEM((SIGNAL, LANES), f32),
        ],
        compiler_params=params,
        name="late_conv",
    )(pltpu.with_memory_space_constraint(taps, pltpu.HBM), skip, pair, value, dmix)


def late_fgrad(pair, mix):
    return pl.pallas_call(
        fgrad_kernel,
        grid=(GROUP,),
        in_specs=[pair_spec, whole((SIGNAL, LANES))],
        out_specs=whole((GROUP, TAPS)),
        out_shape=jax.ShapeDtypeStruct((GROUP, TAPS), f32),
        scratch_shapes=[
            pltpu.VMEM((SIGNAL, LANES), f32),
            pltpu.VMEM((SIGNAL + LANES, LANES), f32),
            pltpu.VMEM((SEQS, 2 * ROWS, LANES), bf16),
            pltpu.VMEM((LANES, WIDE), f32),
            pltpu.VMEM((BLOCKS + 1, GROUP * GROUP, LANES), f32),
        ],
        compiler_params=params,
        name="late_fgrad",
    )(pair, mix)


def swap(values, axes, groups=None):
    return lax.all_to_all(values, axes, split_axis=0, concat_axis=0, tiled=True, axis_index_groups=groups)


def per_device(inputs, value_weight, query, key, filters, skip, cotangent):
    quarter = lax.axis_index("dp")
    side = lax.axis_index("context") % 2

    place = jnp.stack([side, quarter % 2, quarter // 2]).astype(jnp.int32)

    near = [[seq * BLOCKS + 2 * k + place for seq, place in NEAR] for k in range(BLOCKS // 2)]
    tokens = lax.all_gather(inputs[0], ("dp", "context"), axis=0, tiled=True, axis_index_groups=near)
    own_filters = lax.dynamic_slice_in_dim(filters, quarter * GROUP, GROUP, 0)
    own_skip = lax.dynamic_slice_in_dim(skip, quarter * GROUP, GROUP, 0)
    taps = build_taps(own_filters)

    packed = pack(quarter.astype(jnp.int32)[None], value_weight)
    weight = swap(packed.reshape(BLOCKS, value_weight.shape[0], 4 * LANES), "context").reshape(SPAN, 4 * LANES)

    query_part = query[0].astype(f32)
    upstream = cotangent[0].astype(f32)
    dconv = (upstream * query_part).astype(bf16)
    pair = jnp.concatenate([dconv.reshape(ROWS, 1, GROUP, LANES), key[0].reshape(ROWS, 1, GROUP, LANES)], axis=1)
    pair, weight, taps = lax.optimization_barrier((pair, weight, taps))
    pair = swap(pair, ("context", "dp")).reshape(2 * SIGNAL, LANES)

    column = lax.axis_index("tensor").astype(jnp.int32)[None]
    *parts, low, high = project(column, weight, tokens)
    parts = [parts[0]] + [
        lax.ppermute(parts[step], "tensor", [(i, (i + step) % 4) for i in range(4)]) for step in (1, 2, 3)
    ]
    twins = [(k, k ^ 1) for k in range(BLOCKS)]
    other_low = lax.ppermute(low, "context", twins)
    dmix, dvalue = early_dmix(taps, own_skip, pair)
    dvalue, other_low = lax.optimization_barrier((dvalue, other_low))

    both, high = lax.optimization_barrier((join(parts, dvalue), high))
    other_high = lax.ppermute(high, "context", twins)
    both = swap(both.reshape(BLOCKS, HALF, SEQS * LANES), "context")
    dvalue = lax.all_gather(both[:, GROUP:].reshape(BLOCKS * GROUP, SEQS * LANES), "tensor", axis=0, tiled=True)
    out, mix = late_conv(taps, own_skip, pair, both.reshape(BLOCKS * HALF, SEQS * LANES), dmix)
    out = swap(out.reshape(ROWS, 2, GROUP, LANES), ("context", "dp"))
    fgrad = late_fgrad(pair, mix)
    dvalue, fgrad = lax.optimization_barrier((dvalue, fgrad))

    sent, kept = back(place, dvalue, (low, high, other_low, other_high), fgrad)
    received = lax.ppermute(sent, "dp", [(i, i ^ 1) for i in range(SEQS)])
    sent, rest = middle(place, kept, received, fgrad)
    received = lax.ppermute(sent, "dp", [(i, i ^ 2) for i in range(SEQS)])
    input_grad, filter_grad = last(place, rest, received)
    skip_grad = filter_grad[:, 0]

    conv = out[:, 0].reshape(SIGNAL, LANES).astype(f32)
    key_grad = out[:, 1].reshape(SIGNAL, LANES)
    gated = (query_part * conv).astype(bf16)
    query_grad = (upstream * conv).astype(bf16)
    return (gated[None], query_grad[None], key_grad[None], input_grad[None], filter_grad, skip_grad)


def solution(mesh):
    by_channel = P("dp", "tensor", "context")
    by_row = P(("tensor", "context"), None)
    in_specs = (
        P("dp", "context", "tensor"),
        by_row,
        by_channel,
        by_channel,
        by_row,
        P(("tensor", "context")),
        by_channel,
    )
    out_specs = (
        by_channel,
        by_channel,
        by_channel,
        P("dp", "context", "tensor"),
        by_row,
        P(("tensor", "context")),
    )
    return jax.shard_map(
        per_device, mesh=mesh, in_specs=in_specs, out_specs=out_specs, check_vma=False
    )
```

```python
import jax
import jax.numpy as jnp
from jax import lax
from jax.experimental import pallas as pl
from jax.experimental.pallas import tpu as pltpu
from jax.sharding import PartitionSpec as P

f32 = jnp.float32
bf16 = jnp.bfloat16

LANES = 128
GROUP = 8
SEQS = 4
BLOCKS = 32
ROWS = BLOCKS * SEQS
SIGNAL = ROWS * GROUP
TAPS = BLOCKS * LANES
WIDE = TAPS + LANES
DMIX, CONV, FGRAD = 1, 2, 8
NEAR = ((0, 0), (1, 0), (3, 0), (2, 0), (2, 1), (3, 1), (1, 1), (0, 1))
HALF = 16
SPAN = 1024


def pack_kernel(quarter_ref, weight_ref, out_ref, picks):
    @pl.when(pl.program_id(0) == 0)
    def _():
        source = lax.broadcasted_iota(jnp.int32, (SPAN, 2 * LANES), 0)
        target = lax.broadcasted_iota(jnp.int32, (SPAN, 2 * LANES), 1)
        wanted = (target % LANES // 4) * 32 + quarter_ref[0] * GROUP + (target // LANES) * 4 + target % 4
        chosen = (source == wanted).astype(f32).astype(bf16)
        for part in range(4):
            columns = weight_ref[:, part * SPAN : (part + 1) * SPAN]
            picked = jnp.dot(columns, chosen, preferred_element_type=f32).astype(bf16)
            for side in range(2):
                picks[side, :, part * LANES : (part + 1) * LANES] = picked[:, side * LANES : (side + 1) * LANES]

    count = picks.shape[1]
    for dest in range(out_ref.shape[0] // count):
        out_ref[dest * count : (dest + 1) * count, :] = picks[dest % 2]


def load_pair(pair_ref):
    both = pair_ref[...].astype(f32).reshape(ROWS, 2, GROUP, LANES)
    return both[:, 0].reshape(SIGNAL, LANES), both[:, 1].reshape(SIGNAL, LANES)


def taps_kernel(filters_ref, taps_ref, rolled):
    chan = pl.program_id(0)

    @pl.when(chan == 0)
    def _():
        padded = jnp.concatenate([filters_ref[...], jnp.zeros((GROUP, LANES), f32)], axis=1)
        for row in range(GROUP):
            turned = pltpu.roll(padded, row, 1) if row else padded
            for block in range(BLOCKS + 1):
                rolled[block, row * GROUP : (row + 1) * GROUP, :] = turned[:, block * LANES : (block + 1) * LANES]

    base = jnp.concatenate(
        [rolled[block, pl.ds(chan, GROUP, stride=GROUP), :] for block in range(BLOCKS + 1)], axis=1
    )
    for pair in range(LANES // 16):
        low = pltpu.roll(base, 16 * pair, 1) if pair else base
        high = pltpu.roll(base, 16 * pair + 8, 1)
        tile = jnp.concatenate([low[:, :TAPS], high[:, :TAPS]], axis=0).astype(bf16)
        for block in range(BLOCKS):
            taps_ref[0, block * LANES + 16 * pair : block * LANES + 16 * pair + 16, :] = tile[
                :, block * LANES : (block + 1) * LANES
            ]


def fill_ahead(grads, copies, chan):
    for part in range(SEQS):
        copies[part, 0:ROWS, :] = grads[pl.ds(part * SEQS * GROUP + chan, ROWS, stride=GROUP), :].astype(bf16)


def ahead_of(copies, block):
    return copies[block % 4, block // 4 * 16 : block // 4 * 16 + ROWS, :]


def clear_ahead(grads, copies, dconv):
    grads[0:SIGNAL, :] = dconv
    grads[SIGNAL:, :] = jnp.zeros((LANES, LANES), f32)
    for copy in copies:
        for part in range(SEQS):
            copy[part, ROWS:, :] = jnp.zeros((ROWS, LANES), bf16)


def start_taps(taps_ref, taps, done):
    for chan in range(GROUP):
        pltpu.make_async_copy(taps_ref.at[chan], taps.at[chan], done.at[chan]).start()


def wait_taps(taps_ref, taps, done, chan):
    pltpu.make_async_copy(taps_ref.at[chan], taps.at[chan], done.at[chan]).wait()


def dmix_kernel(taps_ref, skip_ref, pair_ref, dmix_ref, dvalue_ref, taps, done, grads, result, *copies):
    step = pl.program_id(0)

    @pl.when(step == 0)
    def _():
        start_taps(taps_ref, taps, done)
        clear_ahead(grads, copies, load_pair(pair_ref)[0])

    for index, copy in enumerate(copies):
        chan = step * DMIX + index
        fill_ahead(grads, copy, chan)
        ahead = jnp.concatenate([ahead_of(copy, block) for block in range(BLOCKS)], axis=1)
        wait_taps(taps_ref, taps, done, chan)
        wide = jnp.concatenate([taps[chan, block * LANES : (block + 1) * LANES, :] for block in range(BLOCKS)], axis=1)
        total = lax.dot_general(ahead, wide, (((1,), (1,)), ((), ())), preferred_element_type=f32)
        own = grads[pl.ds(chan, ROWS, stride=GROUP), :]
        result[pl.ds(chan, ROWS, stride=GROUP), :] = total + skip_ref[chan] * own

    @pl.when(step == pl.num_programs(0) - 1)
    def _():
        _, key = load_pair(pair_ref)
        dmix = result[...].astype(bf16)
        dmix_ref[...] = dmix
        dvalue = (dmix.astype(f32) * key).reshape(BLOCKS, SEQS, GROUP, LANES)
        for seq in range(SEQS):
            dvalue_ref[:, seq * LANES : (seq + 1) * LANES] = (
                dvalue[:, seq].reshape(BLOCKS * GROUP, LANES).astype(bf16)
            )


def project_kernel(column_ref, weight_ref, tokens_ref, out0, out1, out2, out3, turned):
    @pl.when(pl.program_id(0) == 0)
    def _():
        for step in range(4):
            lanes = pl.ds(pl.multiple_of((column_ref[0] + step) % 4 * LANES, LANES), LANES)
            turned[step * LANES : (step + 1) * LANES, :] = weight_ref[:, lanes].T

    product = lax.dot_general(turned[...], tokens_ref[...], (((1,), (1,)), ((), ())), preferred_element_type=f32)
    product = product.astype(bf16)
    for step, out_ref in enumerate((out0, out1, out2, out3)):
        out_ref[...] = product[step * LANES : (step + 1) * LANES, :]


def halves_of(even, odd):
    upper = lax.broadcasted_iota(jnp.int32, even.shape, 0) < 4
    return jnp.where(upper, even, pltpu.roll(odd, 4, 0)), jnp.where(upper, pltpu.roll(even, 4, 0), odd)


def join_kernel(part0, part1, part2, part3, dvalue_ref, out_ref):
    value = part0[...].astype(f32) + part1[...].astype(f32) + part2[...].astype(f32) + part3[...].astype(f32)
    value = value.astype(bf16).astype(f32)
    dvalue = dvalue_ref[...].astype(f32)
    sides = []
    for side in range(2):
        order = [NEAR.index((seq, side)) for seq in range(SEQS)]
        sides.append(jnp.concatenate([value[:, piece * LANES : (piece + 1) * LANES] for piece in order], axis=1))
    for two in range(BLOCKS // 2):
        rows = [part[two * GROUP : (two + 1) * GROUP, :] for part in sides]
        for place, tile in enumerate(halves_of(*rows)):
            index = 2 * two + place
            tile = jnp.concatenate([tile, dvalue[index * GROUP : (index + 1) * GROUP, :]], axis=0)
            out_ref[index * HALF : (index + 1) * HALF, :] = tile.astype(bf16)


def back_kernel(place_ref, dvalue_ref, weights_ref, sent_ref, kept_ref, total):
    index = pl.program_id(0)
    dvalue = dvalue_ref[...].astype(f32)
    tiles = [[], []]
    for two in range(BLOCKS // 2):
        start = two * HALF
        pair = halves_of(dvalue[start : start + GROUP, :], dvalue[start + GROUP : start + HALF, :])
        for half in range(2):
            tiles[half].append(pair[half])
    rows = jnp.concatenate([jnp.concatenate(part, axis=0).astype(bf16) for part in tiles], axis=0)
    columns = jnp.concatenate([weights_ref[0:SPAN, :], weights_ref[SPAN:, :]], axis=1)
    term = lax.dot_general(rows, columns, (((0,), (1,)), ((), ())), preferred_element_type=f32)

    @pl.when(index == 0)
    def _():
        total[...] = term

    @pl.when(index > 0)
    def _():
        total[...] += term

    @pl.when(index == 3)
    def _():
        core = place_ref[1]
        for chip in range(2):
            rows = slice(chip * LANES, (chip + 1) * LANES)
            sent_ref[rows, :] = total[pl.ds((2 * chip + 1 - core) * LANES, LANES), :].astype(bf16)
            kept_ref[rows, :] = total[pl.ds((2 * chip + core) * LANES, LANES), :]


def middle_kernel(place_ref, kept_ref, received_ref, sent_ref, rest_ref):
    chip = place_ref[2]
    for target, index in ((sent_ref, 1 - chip), (rest_ref, chip)):
        rows = pl.ds(pl.multiple_of(index * LANES, LANES), LANES)
        target[...] = (kept_ref[rows, :] + received_ref[rows, :].astype(f32)).astype(bf16)


def last_kernel(place_ref, rest_ref, received_ref, near_ref, far_ref, grad_ref, fgrad_ref, skip_ref):
    grad_ref[...] = (rest_ref[...].astype(f32) + received_ref[...].astype(f32)).astype(bf16)
    pieces = []
    for ref in (near_ref, far_ref):
        both = ref[...].astype(f32)
        pieces += [both[0 : 4 * GROUP, :], both[4 * GROUP :, :]]
    for bit, flag in ((1, place_ref[1]), (2, place_ref[2])):
        pieces = [jnp.where(flag == 0, pieces[index], pieces[index ^ bit]) for index in range(SEQS)]
    for index, piece in enumerate(pieces):
        for part in range(4):
            rows = slice(part * GROUP, (part + 1) * GROUP)
            fgrad_ref[index * GROUP : (index + 1) * GROUP, part * SPAN : (part + 1) * SPAN] = piece[rows, :]
    shape = (SEQS * GROUP, LANES)
    diagonal = lax.broadcasted_iota(jnp.int32, shape, 0) == lax.broadcasted_iota(jnp.int32, shape, 1)
    lag0 = jnp.broadcast_to(fgrad_ref[:, 0:1], shape)
    skip_ref[...] = jnp.sum(jnp.where(diagonal, lag0, 0.0), axis=0, keepdims=True)


def conv_kernel(taps_ref, skip_ref, pair_ref, value_ref, dmix_ref, out_ref, mix_ref, taps, done, mixes, values, result, *copies):
    step = pl.program_id(0)

    @pl.when(step == 0)
    def _():
        start_taps(taps_ref, taps, done)
        _, key = load_pair(pair_ref)
        value = value_ref[...].astype(f32)
        for two in range(BLOCKS // 2):
            start = two * 2 * HALF
            pair = halves_of(value[start : start + GROUP, :], value[start + HALF : start + HALF + GROUP, :])
            for side in range(2):
                for seq in range(SEQS):
                    row = ((2 * two + side) * SEQS + seq) * GROUP
                    values[row : row + GROUP, :] = pair[side][:, seq * LANES : (seq + 1) * LANES]
        mix = (key * values[...]).astype(bf16)
        mix_ref[...] = mix
        mixes[0:LANES, :] = jnp.zeros((LANES, LANES), f32)
        mixes[LANES:, :] = mix.astype(f32)
        for copy in copies:
            for part in range(SEQS):
                copy[part, 0:ROWS, :] = jnp.zeros((ROWS, LANES), bf16)

    for index, copy in enumerate(copies):
        chan = step * CONV + index
        for part in range(SEQS):
            copy[part, ROWS:, :] = mixes[
                pl.ds(LANES - part * SEQS * GROUP + chan, ROWS, stride=GROUP), :
            ].astype(bf16)
        behind = [
            copy[block % 4, ROWS - block // 4 * 16 : 2 * ROWS - block // 4 * 16, :] for block in range(BLOCKS)
        ]
        own = mixes[pl.ds(LANES + chan, ROWS, stride=GROUP), :]
        wait_taps(taps_ref, taps, done, chan)
        total = jnp.dot(jnp.concatenate(behind, axis=1), taps[chan], preferred_element_type=f32)
        result[pl.ds(chan, ROWS, stride=GROUP), :] = total + skip_ref[chan] * own

    @pl.when(step == pl.num_programs(0) - 1)
    def _():
        kgrad = dmix_ref[...].astype(f32) * values[...]
        both = [result[...].reshape(ROWS, 1, GROUP, LANES), kgrad.reshape(ROWS, 1, GROUP, LANES)]
        out_ref[...] = jnp.concatenate(both, axis=1).reshape(2 * SIGNAL, LANES).astype(bf16)


def fgrad_kernel(pair_ref, mix_ref, fgrad_ref, mixes, grads, sums, *scratch):
    step = pl.program_id(0)
    copies, corrs = scratch[:FGRAD], scratch[FGRAD:]

    @pl.when(step == 0)
    def _():
        clear_ahead(grads, copies, load_pair(pair_ref)[0])
        mixes[...] = mix_ref[...].astype(f32)
        for corr in corrs:
            corr[:, TAPS:] = jnp.zeros((LANES, LANES), f32)

    for index, (copy, corr) in enumerate(zip(copies, corrs)):
        chan = step * FGRAD + index
        fill_ahead(grads, copy, chan)
        own = mixes[pl.ds(chan, ROWS, stride=GROUP), :].T.astype(bf16)
        for block in range(0, BLOCKS, 2):
            two = jnp.concatenate([ahead_of(copy, block), ahead_of(copy, block + 1)], axis=1)
            corr[:, block * LANES : (block + 2) * LANES] = jnp.dot(own, two, preferred_element_type=f32)
    for index, corr in enumerate(corrs):
        chan = step * FGRAD + index
        acc = corr[0:GROUP, :]
        for group in range(1, LANES // GROUP):
            acc = acc + pltpu.roll(corr[group * GROUP : (group + 1) * GROUP, :], WIDE - group * GROUP, 1)
        rows = pl.ds(pl.multiple_of(chan * GROUP, GROUP), GROUP)
        for block in range(BLOCKS + 1):
            sums[block, rows, :] = acc[:, block * LANES : (block + 1) * LANES]

    @pl.when(step == pl.num_programs(0) - 1)
    def _():
        fgrad = None
        for row in range(GROUP):
            part = jnp.concatenate(
                [sums[block, pl.ds(row, GROUP, stride=GROUP), :] for block in range(BLOCKS + 1)], axis=1
            )
            fgrad = part if row == 0 else fgrad + pltpu.roll(part, WIDE - row, 1)
        parts = [fgrad[:, part * SPAN : (part + 1) * SPAN] for part in range(4)]
        fgrad_ref[...] = jnp.concatenate(parts, axis=0).astype(bf16)


def whole(shape):
    return pl.BlockSpec(shape, lambda chan: (0,) * len(shape))


params = pltpu.CompilerParams(vmem_limit_bytes=24 * 1024 * 1024)
smem = pl.BlockSpec(memory_space=pltpu.SMEM)
taps_spec = pl.BlockSpec((1, TAPS, LANES), lambda chan: (chan, 0, 0))
any_spec = pl.BlockSpec(memory_space=pl.ANY)
taps_scratch = [pltpu.VMEM((GROUP, TAPS, LANES), bf16), pltpu.SemaphoreType.DMA((GROUP,))]
pair_spec = whole((2 * SIGNAL, LANES))


def pack(quarter, weight):
    steps, rows = 4, weight.shape[0]
    return pl.pallas_call(
        pack_kernel,
        grid=(steps,),
        in_specs=[smem, pl.BlockSpec(weight.shape, lambda step: (0, 0))],
        out_specs=pl.BlockSpec((rows * BLOCKS // steps, 4 * LANES), lambda step: (step, 0)),
        out_shape=jax.ShapeDtypeStruct((rows * BLOCKS, 4 * LANES), bf16),
        scratch_shapes=[pltpu.VMEM((2, rows, 4 * LANES), bf16)],
        compiler_params=params,
        name="pack",
    )(quarter, pltpu.with_memory_space_constraint(weight, pltpu.HBM))


def build_taps(filters):
    return pl.pallas_call(
        taps_kernel,
        grid=(GROUP,),
        in_specs=[whole((GROUP, TAPS))],
        out_specs=taps_spec,
        out_shape=jax.ShapeDtypeStruct((GROUP, TAPS, LANES), bf16),
        scratch_shapes=[pltpu.VMEM((BLOCKS + 1, GROUP * GROUP, LANES), f32)],
        compiler_params=params,
        name="build_taps",
    )(filters)


def early_dmix(taps, skip, pair):
    return pl.pallas_call(
        dmix_kernel,
        grid=(GROUP // DMIX,),
        in_specs=[any_spec, smem, pair_spec],
        out_specs=[whole((SIGNAL, LANES)), whole((BLOCKS * GROUP, SEQS * LANES))],
        out_shape=[
            jax.ShapeDtypeStruct((SIGNAL, LANES), bf16),
            jax.ShapeDtypeStruct((BLOCKS * GROUP, SEQS * LANES), bf16),
        ],
        scratch_shapes=taps_scratch
        + [
            pltpu.VMEM((SIGNAL + LANES, LANES), f32),
            pltpu.VMEM((SIGNAL, LANES), f32),
        ]
        + [pltpu.VMEM((SEQS, 2 * ROWS, LANES), bf16)] * DMIX,
        compiler_params=params,
        name="early_dmix",
    )(pltpu.with_memory_space_constraint(taps, pltpu.HBM), skip, pair)


def project(column, weight, tokens):
    count, steps = tokens.shape[0], 4
    return pl.pallas_call(
        project_kernel,
        grid=(steps,),
        in_specs=[smem, whole(weight.shape), pl.BlockSpec((count // steps, SPAN), lambda step: (step, 0))],
        out_specs=[pl.BlockSpec((LANES, count // steps), lambda step: (0, step))] * 4,
        out_shape=[jax.ShapeDtypeStruct((LANES, count), bf16)] * 4,
        scratch_shapes=[pltpu.VMEM((4 * LANES, SPAN), bf16)],
        compiler_params=params,
        name="project",
    )(column, *[pltpu.with_memory_space_constraint(x, pltpu.HBM) for x in (weight, tokens)])


def vmem_specs(count):
    return [smem] + [pl.BlockSpec(memory_space=pltpu.VMEM)] * count


def join(parts, dvalue):
    return pl.pallas_call(
        join_kernel,
        out_shape=jax.ShapeDtypeStruct((BLOCKS * HALF, SEQS * LANES), bf16),
        compiler_params=params,
        name="join",
    )(*parts, dvalue)


def back(place, dvalue, weights):
    return pl.pallas_call(
        back_kernel,
        grid=(4,),
        in_specs=[
            smem,
            pl.BlockSpec((BLOCKS * GROUP, SEQS * LANES), lambda step: (step, 0)),
            pl.BlockSpec((2 * SPAN, LANES), lambda step: (0, step)),
        ],
        out_specs=[whole((2 * LANES, SPAN)), whole((2 * LANES, SPAN))],
        out_shape=[
            jax.ShapeDtypeStruct((2 * LANES, SPAN), bf16),
            jax.ShapeDtypeStruct((2 * LANES, SPAN), f32),
        ],
        scratch_shapes=[pltpu.VMEM((SEQS * LANES, SPAN), f32)],
        compiler_params=params,
        name="back",
    )(place, *[pltpu.with_memory_space_constraint(x, pltpu.HBM) for x in (dvalue, weights)])


def middle(place, kept, received):
    return pl.pallas_call(
        middle_kernel,
        in_specs=vmem_specs(2),
        out_shape=[jax.ShapeDtypeStruct((LANES, SPAN), bf16)] * 2,
        compiler_params=params,
        name="middle",
    )(place, kept, received)


def last(place, rest, received, near, far):
    return pl.pallas_call(
        last_kernel,
        in_specs=vmem_specs(4),
        out_shape=[
            jax.ShapeDtypeStruct((LANES, SPAN), bf16),
            jax.ShapeDtypeStruct((2 * HALF, TAPS), f32),
            jax.ShapeDtypeStruct((1, LANES), f32),
        ],
        compiler_params=params,
        name="last",
    )(place, rest, received, near, far)


def late_conv(taps, skip, pair, value, dmix):
    return pl.pallas_call(
        conv_kernel,
        grid=(GROUP // CONV,),
        in_specs=[
            any_spec,
            smem,
            pair_spec,
            whole((BLOCKS * HALF, SEQS * LANES)),
            whole((SIGNAL, LANES)),
        ],
        out_specs=[whole((2 * SIGNAL, LANES)), whole((SIGNAL, LANES))],
        out_shape=[
            jax.ShapeDtypeStruct((2 * SIGNAL, LANES), bf16),
            jax.ShapeDtypeStruct((SIGNAL, LANES), bf16),
        ],
        scratch_shapes=taps_scratch
        + [
            pltpu.VMEM((SIGNAL + LANES, LANES), f32),
            pltpu.VMEM((SIGNAL, LANES), f32),
            pltpu.VMEM((SIGNAL, LANES), f32),
        ]
        + [pltpu.VMEM((SEQS, 2 * ROWS, LANES), bf16)] * CONV,
        compiler_params=params,
        name="late_conv",
    )(pltpu.with_memory_space_constraint(taps, pltpu.HBM), skip, pair, value, dmix)


def late_fgrad(pair, mix):
    return pl.pallas_call(
        fgrad_kernel,
        grid=(GROUP // FGRAD,),
        in_specs=[pair_spec, whole((SIGNAL, LANES))],
        out_specs=whole((4 * GROUP, SPAN)),
        out_shape=jax.ShapeDtypeStruct((4 * GROUP, SPAN), bf16),
        scratch_shapes=[
            pltpu.VMEM((SIGNAL, LANES), f32),
            pltpu.VMEM((SIGNAL + LANES, LANES), f32),
            pltpu.VMEM((BLOCKS + 1, GROUP * GROUP, LANES), f32),
        ]
        + [pltpu.VMEM((SEQS, 2 * ROWS, LANES), bf16)] * FGRAD
        + [pltpu.VMEM((LANES, WIDE), f32)] * FGRAD,
        compiler_params=params,
        name="late_fgrad",
    )(pair, mix)


def swap(values, axes, groups=None):
    return lax.all_to_all(values, axes, split_axis=0, concat_axis=0, tiled=True, axis_index_groups=groups)


def per_device(inputs, value_weight, query, key, filters, skip, cotangent):
    quarter = lax.axis_index("dp")
    side = lax.axis_index("context") % 2

    place = jnp.stack([side, quarter % 2, quarter // 2]).astype(jnp.int32)

    near = [[seq * BLOCKS + 2 * k + place for seq, place in NEAR] for k in range(BLOCKS // 2)]
    tokens = lax.all_gather(inputs[0], ("dp", "context"), axis=0, tiled=True, axis_index_groups=near)
    own_filters = lax.dynamic_slice_in_dim(filters, quarter * GROUP, GROUP, 0)
    own_skip = lax.dynamic_slice_in_dim(skip, quarter * GROUP, GROUP, 0)
    taps = build_taps(own_filters)

    packed = pack(quarter.astype(jnp.int32)[None], value_weight)
    weight = swap(packed.reshape(BLOCKS, value_weight.shape[0], 4 * LANES), "context").reshape(SPAN, 4 * LANES)

    query_part = query[0].astype(f32)
    upstream = cotangent[0].astype(f32)
    dconv = (upstream * query_part).astype(bf16)
    pair = jnp.concatenate([dconv.reshape(ROWS, 1, GROUP, LANES), key[0].reshape(ROWS, 1, GROUP, LANES)], axis=1)
    pair, weight, taps = lax.optimization_barrier((pair, weight, taps))
    pair = swap(pair, ("context", "dp")).reshape(2 * SIGNAL, LANES)

    column = lax.axis_index("tensor").astype(jnp.int32)[None]
    parts = project(column, weight, tokens)
    parts = [parts[0]] + [
        lax.ppermute(parts[step], "tensor", [(i, (i + step) % 4) for i in range(4)]) for step in (1, 2, 3)
    ]
    sides = [[2 * k, 2 * k + 1] for k in range(BLOCKS // 2)]
    weights = lax.all_gather(weight, "context", axis=0, tiled=True, axis_index_groups=sides)
    dmix, dvalue = early_dmix(taps, own_skip, pair)

    both = swap(join(parts, dvalue).reshape(BLOCKS, HALF, SEQS * LANES), "context")
    both, weights = lax.optimization_barrier((both, weights))
    dvalue = lax.all_gather(both[:, GROUP:].reshape(BLOCKS * GROUP, SEQS * LANES), "tensor", axis=0, tiled=True)
    out, mix = late_conv(taps, own_skip, pair, both.reshape(BLOCKS * HALF, SEQS * LANES), dmix)
    out = swap(out.reshape(ROWS, 2, GROUP, LANES), ("context", "dp"))
    fgrad = late_fgrad(pair, mix)

    def cross(values, bit):
        return lax.ppermute(values, "dp", [(i, i ^ bit) for i in range(SEQS)])

    place = jnp.stack([side, quarter % 2, quarter // 2]).astype(jnp.int32)
    chip_fgrads = jnp.concatenate([fgrad, cross(fgrad, 1)], axis=0)
    far_fgrads = cross(chip_fgrads, 2)
    dvalue, chip_fgrads = lax.optimization_barrier((dvalue, chip_fgrads))
    sent, kept = back(place, dvalue, weights)
    sent, rest = middle(place, kept, cross(sent, 1))
    input_grad, filter_grad, skip_grad = last(place, rest, cross(sent, 2), chip_fgrads, far_fgrads)
    skip_grad = skip_grad[0, : skip.shape[0]]

    conv = out[:, 0].reshape(SIGNAL, LANES).astype(f32)
    key_grad = out[:, 1].reshape(SIGNAL, LANES)
    gated = (query_part * conv).astype(bf16)
    query_grad = (upstream * conv).astype(bf16)
    return (gated[None], query_grad[None], key_grad[None], input_grad[None], filter_grad, skip_grad)


def solution(mesh):
    by_channel = P("dp", "tensor", "context")
    by_row = P(("tensor", "context"), None)
    in_specs = (
        P("dp", "context", "tensor"),
        by_row,
        by_channel,
        by_channel,
        by_row,
        P(("tensor", "context")),
        by_channel,
    )
    out_specs = (
        by_channel,
        by_channel,
        by_channel,
        P("dp", "context", "tensor"),
        by_row,
        P(("tensor", "context")),
    )
    return jax.shard_map(
        per_device, mesh=mesh, in_specs=in_specs, out_specs=out_specs, check_vma=False
    )
```

```python
import jax
import jax.numpy as jnp
from jax import lax
from jax.experimental import pallas as pl
from jax.experimental.pallas import tpu as pltpu
from jax.sharding import PartitionSpec as P

f32 = jnp.float32
bf16 = jnp.bfloat16

LANES = 128
GROUP = 8
SEQS = 4
BLOCKS = 32
ROWS = BLOCKS * SEQS
SIGNAL = ROWS * GROUP
TAPS = BLOCKS * LANES
WIDE = TAPS + LANES
DMIX, CONV, FGRAD = 1, 2, 8
NEAR = ((0, 0), (1, 0), (3, 0), (2, 0), (2, 1), (3, 1), (1, 1), (0, 1))
HALF = 16
SPAN = 1024


def pack_kernel(quarter_ref, weight_ref, out_ref, picks):
    @pl.when(pl.program_id(0) == 0)
    def _():
        source = lax.broadcasted_iota(jnp.int32, (SPAN, 2 * LANES), 0)
        target = lax.broadcasted_iota(jnp.int32, (SPAN, 2 * LANES), 1)
        wanted = (target % LANES // 4) * 32 + quarter_ref[0] * GROUP + (target // LANES) * 4 + target % 4
        chosen = (source == wanted).astype(f32).astype(bf16)
        for part in range(4):
            columns = weight_ref[:, part * SPAN : (part + 1) * SPAN]
            picked = jnp.dot(columns, chosen, preferred_element_type=f32).astype(bf16)
            for side in range(2):
                picks[side, :, part * LANES : (part + 1) * LANES] = picked[:, side * LANES : (side + 1) * LANES]

    count = picks.shape[1]
    for dest in range(out_ref.shape[0] // count):
        out_ref[dest * count : (dest + 1) * count, :] = picks[dest % 2]


def load_pair(pair_ref):
    both = pair_ref[...].astype(f32).reshape(ROWS, 2, GROUP, LANES)
    return both[:, 0].reshape(SIGNAL, LANES), both[:, 1].reshape(SIGNAL, LANES)


def taps_kernel(filters_ref, taps_ref, rolled):
    chan = pl.program_id(0)

    @pl.when(chan == 0)
    def _():
        padded = jnp.concatenate([filters_ref[...], jnp.zeros((GROUP, LANES), f32)], axis=1)
        for row in range(GROUP):
            turned = pltpu.roll(padded, row, 1) if row else padded
            for block in range(BLOCKS + 1):
                rolled[block, row * GROUP : (row + 1) * GROUP, :] = turned[:, block * LANES : (block + 1) * LANES]

    base = jnp.concatenate(
        [rolled[block, pl.ds(chan, GROUP, stride=GROUP), :] for block in range(BLOCKS + 1)], axis=1
    )
    for pair in range(LANES // 16):
        low = pltpu.roll(base, 16 * pair, 1) if pair else base
        high = pltpu.roll(base, 16 * pair + 8, 1)
        tile = jnp.concatenate([low[:, :TAPS], high[:, :TAPS]], axis=0).astype(bf16)
        for block in range(BLOCKS):
            taps_ref[0, block * LANES + 16 * pair : block * LANES + 16 * pair + 16, :] = tile[
                :, block * LANES : (block + 1) * LANES
            ]


def fill_ahead(grads, copies, chan):
    for part in range(SEQS):
        copies[part, 0:ROWS, :] = grads[pl.ds(part * SEQS * GROUP + chan, ROWS, stride=GROUP), :].astype(bf16)


def ahead_of(copies, block):
    return copies[block % 4, block // 4 * 16 : block // 4 * 16 + ROWS, :]


def clear_ahead(grads, copies, dconv):
    grads[0:SIGNAL, :] = dconv
    grads[SIGNAL:, :] = jnp.zeros((LANES, LANES), f32)
    for copy in copies:
        for part in range(SEQS):
            copy[part, ROWS:, :] = jnp.zeros((ROWS, LANES), bf16)


def start_taps(taps_ref, taps, done):
    for chan in range(GROUP):
        pltpu.make_async_copy(taps_ref.at[chan], taps.at[chan], done.at[chan]).start()


def wait_taps(taps_ref, taps, done, chan):
    pltpu.make_async_copy(taps_ref.at[chan], taps.at[chan], done.at[chan]).wait()


def dmix_kernel(taps_ref, skip_ref, pair_ref, dmix_ref, dvalue_ref, taps, done, grads, result, *copies):
    step = pl.program_id(0)

    @pl.when(step == 0)
    def _():
        start_taps(taps_ref, taps, done)
        clear_ahead(grads, copies, load_pair(pair_ref)[0])

    for index, copy in enumerate(copies):
        chan = step * DMIX + index
        fill_ahead(grads, copy, chan)
        ahead = jnp.concatenate([ahead_of(copy, block) for block in range(BLOCKS)], axis=1)
        wait_taps(taps_ref, taps, done, chan)
        wide = jnp.concatenate([taps[chan, block * LANES : (block + 1) * LANES, :] for block in range(BLOCKS)], axis=1)
        total = lax.dot_general(ahead, wide, (((1,), (1,)), ((), ())), preferred_element_type=f32)
        own = grads[pl.ds(chan, ROWS, stride=GROUP), :]
        result[pl.ds(chan, ROWS, stride=GROUP), :] = total + skip_ref[chan] * own

    @pl.when(step == pl.num_programs(0) - 1)
    def _():
        _, key = load_pair(pair_ref)
        dmix = result[...].astype(bf16)
        dmix_ref[...] = dmix
        dvalue = (dmix.astype(f32) * key).reshape(BLOCKS, SEQS, GROUP, LANES)
        for seq in range(SEQS):
            dvalue_ref[:, seq * LANES : (seq + 1) * LANES] = (
                dvalue[:, seq].reshape(BLOCKS * GROUP, LANES).astype(bf16)
            )


def project_kernel(column_ref, weight_ref, tokens_ref, out0, out1, out2, out3, turned):
    @pl.when(pl.program_id(0) == 0)
    def _():
        for step in range(4):
            lanes = pl.ds(pl.multiple_of((column_ref[0] + step) % 4 * LANES, LANES), LANES)
            turned[step * LANES : (step + 1) * LANES, :] = weight_ref[:, lanes].T

    product = lax.dot_general(turned[...], tokens_ref[...], (((1,), (1,)), ((), ())), preferred_element_type=f32)
    product = product.astype(bf16)
    for step, out_ref in enumerate((out0, out1, out2, out3)):
        out_ref[...] = product[step * LANES : (step + 1) * LANES, :]


def halves_of(even, odd):
    upper = lax.broadcasted_iota(jnp.int32, even.shape, 0) < 4
    return jnp.where(upper, even, pltpu.roll(odd, 4, 0)), jnp.where(upper, pltpu.roll(even, 4, 0), odd)


def join_kernel(part0, part1, part2, part3, dvalue_ref, out_ref):
    value = part0[...].astype(f32) + part1[...].astype(f32) + part2[...].astype(f32) + part3[...].astype(f32)
    value = value.astype(bf16).astype(f32)
    dvalue = dvalue_ref[...].astype(f32)
    sides = []
    for side in range(2):
        order = [NEAR.index((seq, side)) for seq in range(SEQS)]
        sides.append(jnp.concatenate([value[:, piece * LANES : (piece + 1) * LANES] for piece in order], axis=1))
    for two in range(BLOCKS // 2):
        rows = [part[two * GROUP : (two + 1) * GROUP, :] for part in sides]
        for place, tile in enumerate(halves_of(*rows)):
            index = 2 * two + place
            tile = jnp.concatenate([tile, dvalue[index * GROUP : (index + 1) * GROUP, :]], axis=0)
            out_ref[index * HALF : (index + 1) * HALF, :] = tile.astype(bf16)


def back_kernel(place_ref, dvalue_ref, own_ref, other_ref, sent_ref, kept_ref, total):
    index = pl.program_id(0)
    dvalue = dvalue_ref[...].astype(f32)
    tiles = [[], []]
    for two in range(BLOCKS // 2):
        start = two * HALF
        pair = halves_of(dvalue[start : start + GROUP, :], dvalue[start + GROUP : start + HALF, :])
        for half in range(2):
            tiles[half].append(pair[half])
    upper, lower = [jnp.concatenate(part, axis=0).astype(bf16) for part in tiles]
    first = place_ref[0] == 0
    rows = jnp.concatenate([jnp.where(first, upper, lower), jnp.where(first, lower, upper)], axis=0)
    columns = jnp.concatenate([own_ref[...], other_ref[...]], axis=1)
    term = lax.dot_general(rows, columns, (((0,), (1,)), ((), ())), preferred_element_type=f32)

    @pl.when(index == 0)
    def _():
        total[...] = term

    @pl.when(index > 0)
    def _():
        total[...] += term

    @pl.when(index == 3)
    def _():
        core = place_ref[1]
        for chip in range(2):
            rows = slice(chip * LANES, (chip + 1) * LANES)
            sent_ref[rows, :] = total[pl.ds((2 * chip + 1 - core) * LANES, LANES), :].astype(bf16)
            kept_ref[rows, :] = total[pl.ds((2 * chip + core) * LANES, LANES), :]


def middle_kernel(place_ref, kept_ref, received_ref, sent_ref, rest_ref):
    chip = place_ref[2]
    for target, index in ((sent_ref, 1 - chip), (rest_ref, chip)):
        rows = pl.ds(pl.multiple_of(index * LANES, LANES), LANES)
        target[...] = (kept_ref[rows, :] + received_ref[rows, :].astype(f32)).astype(bf16)


def last_kernel(place_ref, rest_ref, received_ref, near_ref, far_ref, grad_ref, fgrad_ref, skip_ref):
    grad_ref[...] = (rest_ref[...].astype(f32) + received_ref[...].astype(f32)).astype(bf16)
    pieces = []
    for ref in (near_ref, far_ref):
        both = ref[...].astype(f32)
        pieces += [both[0 : 4 * GROUP, :], both[4 * GROUP :, :]]
    for bit, flag in ((1, place_ref[1]), (2, place_ref[2])):
        pieces = [jnp.where(flag == 0, pieces[index], pieces[index ^ bit]) for index in range(SEQS)]
    for index, piece in enumerate(pieces):
        for part in range(4):
            rows = slice(part * GROUP, (part + 1) * GROUP)
            fgrad_ref[index * GROUP : (index + 1) * GROUP, part * SPAN : (part + 1) * SPAN] = piece[rows, :]
    shape = (SEQS * GROUP, LANES)
    diagonal = lax.broadcasted_iota(jnp.int32, shape, 0) == lax.broadcasted_iota(jnp.int32, shape, 1)
    lag0 = jnp.broadcast_to(fgrad_ref[:, 0:1], shape)
    skip_ref[...] = jnp.sum(jnp.where(diagonal, lag0, 0.0), axis=0, keepdims=True)


def conv_kernel(taps_ref, skip_ref, pair_ref, value_ref, dmix_ref, out_ref, mix_ref, taps, done, mixes, values, result, *copies):
    step = pl.program_id(0)

    @pl.when(step == 0)
    def _():
        start_taps(taps_ref, taps, done)
        _, key = load_pair(pair_ref)
        value = value_ref[...].astype(f32)
        for two in range(BLOCKS // 2):
            start = two * 2 * HALF
            pair = halves_of(value[start : start + GROUP, :], value[start + HALF : start + HALF + GROUP, :])
            for side in range(2):
                for seq in range(SEQS):
                    row = ((2 * two + side) * SEQS + seq) * GROUP
                    values[row : row + GROUP, :] = pair[side][:, seq * LANES : (seq + 1) * LANES]
        mix = (key * values[...]).astype(bf16)
        mix_ref[...] = mix
        mixes[0:LANES, :] = jnp.zeros((LANES, LANES), f32)
        mixes[LANES:, :] = mix.astype(f32)
        for copy in copies:
            for part in range(SEQS):
                copy[part, 0:ROWS, :] = jnp.zeros((ROWS, LANES), bf16)

    for index, copy in enumerate(copies):
        chan = step * CONV + index
        for part in range(SEQS):
            copy[part, ROWS:, :] = mixes[
                pl.ds(LANES - part * SEQS * GROUP + chan, ROWS, stride=GROUP), :
            ].astype(bf16)
        behind = [
            copy[block % 4, ROWS - block // 4 * 16 : 2 * ROWS - block // 4 * 16, :] for block in range(BLOCKS)
        ]
        own = mixes[pl.ds(LANES + chan, ROWS, stride=GROUP), :]
        wait_taps(taps_ref, taps, done, chan)
        total = jnp.dot(jnp.concatenate(behind, axis=1), taps[chan], preferred_element_type=f32)
        result[pl.ds(chan, ROWS, stride=GROUP), :] = total + skip_ref[chan] * own

    @pl.when(step == pl.num_programs(0) - 1)
    def _():
        kgrad = dmix_ref[...].astype(f32) * values[...]
        both = [result[...].reshape(ROWS, 1, GROUP, LANES), kgrad.reshape(ROWS, 1, GROUP, LANES)]
        out_ref[...] = jnp.concatenate(both, axis=1).reshape(2 * SIGNAL, LANES).astype(bf16)


def fgrad_kernel(pair_ref, mix_ref, fgrad_ref, mixes, grads, sums, *scratch):
    step = pl.program_id(0)
    copies, corrs = scratch[:FGRAD], scratch[FGRAD:]

    @pl.when(step == 0)
    def _():
        clear_ahead(grads, copies, load_pair(pair_ref)[0])
        mixes[...] = mix_ref[...].astype(f32)
        for corr in corrs:
            corr[:, TAPS:] = jnp.zeros((LANES, LANES), f32)

    for index, (copy, corr) in enumerate(zip(copies, corrs)):
        chan = step * FGRAD + index
        fill_ahead(grads, copy, chan)
        own = mixes[pl.ds(chan, ROWS, stride=GROUP), :].T.astype(bf16)
        for block in range(0, BLOCKS, 2):
            two = jnp.concatenate([ahead_of(copy, block), ahead_of(copy, block + 1)], axis=1)
            corr[:, block * LANES : (block + 2) * LANES] = jnp.dot(own, two, preferred_element_type=f32)
    for index, corr in enumerate(corrs):
        chan = step * FGRAD + index
        acc = corr[0:GROUP, :]
        for group in range(1, LANES // GROUP):
            acc = acc + pltpu.roll(corr[group * GROUP : (group + 1) * GROUP, :], WIDE - group * GROUP, 1)
        rows = pl.ds(pl.multiple_of(chan * GROUP, GROUP), GROUP)
        for block in range(BLOCKS + 1):
            sums[block, rows, :] = acc[:, block * LANES : (block + 1) * LANES]

    @pl.when(step == pl.num_programs(0) - 1)
    def _():
        fgrad = None
        for row in range(GROUP):
            part = jnp.concatenate(
                [sums[block, pl.ds(row, GROUP, stride=GROUP), :] for block in range(BLOCKS + 1)], axis=1
            )
            fgrad = part if row == 0 else fgrad + pltpu.roll(part, WIDE - row, 1)
        parts = [fgrad[:, part * SPAN : (part + 1) * SPAN] for part in range(4)]
        fgrad_ref[...] = jnp.concatenate(parts, axis=0).astype(bf16)


def whole(shape):
    return pl.BlockSpec(shape, lambda chan: (0,) * len(shape))


params = pltpu.CompilerParams(vmem_limit_bytes=24 * 1024 * 1024)
smem = pl.BlockSpec(memory_space=pltpu.SMEM)
taps_spec = pl.BlockSpec((1, TAPS, LANES), lambda chan: (chan, 0, 0))
any_spec = pl.BlockSpec(memory_space=pl.ANY)
taps_scratch = [pltpu.VMEM((GROUP, TAPS, LANES), bf16), pltpu.SemaphoreType.DMA((GROUP,))]
pair_spec = whole((2 * SIGNAL, LANES))


def pack(quarter, weight):
    steps, rows = 4, weight.shape[0]
    return pl.pallas_call(
        pack_kernel,
        grid=(steps,),
        in_specs=[smem, pl.BlockSpec(weight.shape, lambda step: (0, 0))],
        out_specs=pl.BlockSpec((rows * BLOCKS // steps, 4 * LANES), lambda step: (step, 0)),
        out_shape=jax.ShapeDtypeStruct((rows * BLOCKS, 4 * LANES), bf16),
        scratch_shapes=[pltpu.VMEM((2, rows, 4 * LANES), bf16)],
        compiler_params=params,
        name="pack",
    )(quarter, pltpu.with_memory_space_constraint(weight, pltpu.HBM))


def build_taps(filters):
    return pl.pallas_call(
        taps_kernel,
        grid=(GROUP,),
        in_specs=[whole((GROUP, TAPS))],
        out_specs=taps_spec,
        out_shape=jax.ShapeDtypeStruct((GROUP, TAPS, LANES), bf16),
        scratch_shapes=[pltpu.VMEM((BLOCKS + 1, GROUP * GROUP, LANES), f32)],
        compiler_params=params,
        name="build_taps",
    )(filters)


def early_dmix(taps, skip, pair):
    return pl.pallas_call(
        dmix_kernel,
        grid=(GROUP // DMIX,),
        in_specs=[any_spec, smem, pair_spec],
        out_specs=[whole((SIGNAL, LANES)), whole((BLOCKS * GROUP, SEQS * LANES))],
        out_shape=[
            jax.ShapeDtypeStruct((SIGNAL, LANES), bf16),
            jax.ShapeDtypeStruct((BLOCKS * GROUP, SEQS * LANES), bf16),
        ],
        scratch_shapes=taps_scratch
        + [
            pltpu.VMEM((SIGNAL + LANES, LANES), f32),
            pltpu.VMEM((SIGNAL, LANES), f32),
        ]
        + [pltpu.VMEM((SEQS, 2 * ROWS, LANES), bf16)] * DMIX,
        compiler_params=params,
        name="early_dmix",
    )(pltpu.with_memory_space_constraint(taps, pltpu.HBM), skip, pair)


def project(column, weight, tokens):
    count, steps = tokens.shape[0], 4
    return pl.pallas_call(
        project_kernel,
        grid=(steps,),
        in_specs=[smem, whole(weight.shape), pl.BlockSpec((count // steps, SPAN), lambda step: (step, 0))],
        out_specs=[pl.BlockSpec((LANES, count // steps), lambda step: (0, step))] * 4,
        out_shape=[jax.ShapeDtypeStruct((LANES, count), bf16)] * 4,
        scratch_shapes=[pltpu.VMEM((4 * LANES, SPAN), bf16)],
        compiler_params=params,
        name="project",
    )(column, *[pltpu.with_memory_space_constraint(x, pltpu.HBM) for x in (weight, tokens)])


def vmem_specs(count):
    return [smem] + [pl.BlockSpec(memory_space=pltpu.VMEM)] * count


def join(parts, dvalue):
    return pl.pallas_call(
        join_kernel,
        out_shape=jax.ShapeDtypeStruct((BLOCKS * HALF, SEQS * LANES), bf16),
        compiler_params=params,
        name="join",
    )(*parts, dvalue)


def back(place, dvalue, own, other):
    return pl.pallas_call(
        back_kernel,
        grid=(4,),
        in_specs=[
            smem,
            pl.BlockSpec((BLOCKS * GROUP, SEQS * LANES), lambda step: (step, 0)),
            pl.BlockSpec((SPAN, LANES), lambda step: (0, step)),
            pl.BlockSpec((SPAN, LANES), lambda step: (0, step)),
        ],
        out_specs=[whole((2 * LANES, SPAN)), whole((2 * LANES, SPAN))],
        out_shape=[
            jax.ShapeDtypeStruct((2 * LANES, SPAN), bf16),
            jax.ShapeDtypeStruct((2 * LANES, SPAN), f32),
        ],
        scratch_shapes=[pltpu.VMEM((SEQS * LANES, SPAN), f32)],
        compiler_params=params,
        name="back",
    )(place, *[pltpu.with_memory_space_constraint(x, pltpu.HBM) for x in (dvalue, own, other)])


def middle(place, kept, received):
    return pl.pallas_call(
        middle_kernel,
        in_specs=vmem_specs(2),
        out_shape=[jax.ShapeDtypeStruct((LANES, SPAN), bf16)] * 2,
        compiler_params=params,
        name="middle",
    )(place, kept, received)


def last(place, rest, received, near, far):
    return pl.pallas_call(
        last_kernel,
        in_specs=vmem_specs(4),
        out_shape=[
            jax.ShapeDtypeStruct((LANES, SPAN), bf16),
            jax.ShapeDtypeStruct((2 * HALF, TAPS), f32),
            jax.ShapeDtypeStruct((1, LANES), f32),
        ],
        compiler_params=params,
        name="last",
    )(place, rest, received, near, far)


def late_conv(taps, skip, pair, value, dmix):
    return pl.pallas_call(
        conv_kernel,
        grid=(GROUP // CONV,),
        in_specs=[
            any_spec,
            smem,
            pair_spec,
            whole((BLOCKS * HALF, SEQS * LANES)),
            whole((SIGNAL, LANES)),
        ],
        out_specs=[whole((2 * SIGNAL, LANES)), whole((SIGNAL, LANES))],
        out_shape=[
            jax.ShapeDtypeStruct((2 * SIGNAL, LANES), bf16),
            jax.ShapeDtypeStruct((SIGNAL, LANES), bf16),
        ],
        scratch_shapes=taps_scratch
        + [
            pltpu.VMEM((SIGNAL + LANES, LANES), f32),
            pltpu.VMEM((SIGNAL, LANES), f32),
            pltpu.VMEM((SIGNAL, LANES), f32),
        ]
        + [pltpu.VMEM((SEQS, 2 * ROWS, LANES), bf16)] * CONV,
        compiler_params=params,
        name="late_conv",
    )(pltpu.with_memory_space_constraint(taps, pltpu.HBM), skip, pair, value, dmix)


def late_fgrad(pair, mix):
    return pl.pallas_call(
        fgrad_kernel,
        grid=(GROUP // FGRAD,),
        in_specs=[pair_spec, whole((SIGNAL, LANES))],
        out_specs=whole((4 * GROUP, SPAN)),
        out_shape=jax.ShapeDtypeStruct((4 * GROUP, SPAN), bf16),
        scratch_shapes=[
            pltpu.VMEM((SIGNAL, LANES), f32),
            pltpu.VMEM((SIGNAL + LANES, LANES), f32),
            pltpu.VMEM((BLOCKS + 1, GROUP * GROUP, LANES), f32),
        ]
        + [pltpu.VMEM((SEQS, 2 * ROWS, LANES), bf16)] * FGRAD
        + [pltpu.VMEM((LANES, WIDE), f32)] * FGRAD,
        compiler_params=params,
        name="late_fgrad",
    )(pair, mix)


def swap(values, axes, groups=None):
    return lax.all_to_all(values, axes, split_axis=0, concat_axis=0, tiled=True, axis_index_groups=groups)


def per_device(inputs, value_weight, query, key, filters, skip, cotangent):
    quarter = lax.axis_index("dp")
    side = lax.axis_index("context") % 2

    place = jnp.stack([side, quarter % 2, quarter // 2]).astype(jnp.int32)

    near = [[seq * BLOCKS + 2 * k + place for seq, place in NEAR] for k in range(BLOCKS // 2)]
    tokens = lax.all_gather(inputs[0], ("dp", "context"), axis=0, tiled=True, axis_index_groups=near)
    own_filters = lax.dynamic_slice_in_dim(filters, quarter * GROUP, GROUP, 0)
    own_skip = lax.dynamic_slice_in_dim(skip, quarter * GROUP, GROUP, 0)
    taps = build_taps(own_filters)

    packed = pack(quarter.astype(jnp.int32)[None], value_weight)
    weight = swap(packed.reshape(BLOCKS, value_weight.shape[0], 4 * LANES), "context").reshape(SPAN, 4 * LANES)

    query_part = query[0].astype(f32)
    upstream = cotangent[0].astype(f32)
    dconv = (upstream * query_part).astype(bf16)
    pair = jnp.concatenate([dconv.reshape(ROWS, 1, GROUP, LANES), key[0].reshape(ROWS, 1, GROUP, LANES)], axis=1)
    pair, weight, taps = lax.optimization_barrier((pair, weight, taps))
    pair = swap(pair, ("context", "dp")).reshape(2 * SIGNAL, LANES)

    column = lax.axis_index("tensor").astype(jnp.int32)[None]
    parts = project(column, weight, tokens)
    parts = [parts[0]] + [
        lax.ppermute(parts[step], "tensor", [(i, (i + step) % 4) for i in range(4)]) for step in (1, 2, 3)
    ]
    other = lax.ppermute(weight, "context", [(k, k ^ 1) for k in range(BLOCKS)])
    dmix, dvalue = early_dmix(taps, own_skip, pair)

    both = swap(join(parts, dvalue).reshape(BLOCKS, HALF, SEQS * LANES), "context")
    both, other = lax.optimization_barrier((both, other))
    dvalue = lax.all_gather(both[:, GROUP:].reshape(BLOCKS * GROUP, SEQS * LANES), "tensor", axis=0, tiled=True)
    out, mix = late_conv(taps, own_skip, pair, both.reshape(BLOCKS * HALF, SEQS * LANES), dmix)
    out = swap(out.reshape(ROWS, 2, GROUP, LANES), ("context", "dp"))
    fgrad = late_fgrad(pair, mix)

    def cross(values, bit):
        return lax.ppermute(values, "dp", [(i, i ^ bit) for i in range(SEQS)])

    place = jnp.stack([side, quarter % 2, quarter // 2]).astype(jnp.int32)
    chip_fgrads = jnp.concatenate([fgrad, cross(fgrad, 1)], axis=0)
    far_fgrads = cross(chip_fgrads, 2)
    dvalue, chip_fgrads = lax.optimization_barrier((dvalue, chip_fgrads))
    sent, kept = back(place, dvalue, weight, other)
    sent, rest = middle(place, kept, cross(sent, 1))
    input_grad, filter_grad, skip_grad = last(place, rest, cross(sent, 2), chip_fgrads, far_fgrads)
    skip_grad = skip_grad[0, : skip.shape[0]]

    conv = out[:, 0].reshape(SIGNAL, LANES).astype(f32)
    key_grad = out[:, 1].reshape(SIGNAL, LANES)
    gated = (query_part * conv).astype(bf16)
    query_grad = (upstream * conv).astype(bf16)
    return (gated[None], query_grad[None], key_grad[None], input_grad[None], filter_grad, skip_grad)


def solution(mesh):
    by_channel = P("dp", "tensor", "context")
    by_row = P(("tensor", "context"), None)
    in_specs = (
        P("dp", "context", "tensor"),
        by_row,
        by_channel,
        by_channel,
        by_row,
        P(("tensor", "context")),
        by_channel,
    )
    out_specs = (
        by_channel,
        by_channel,
        by_channel,
        P("dp", "context", "tensor"),
        by_row,
        P(("tensor", "context")),
    )
    return jax.shard_map(
        per_device, mesh=mesh, in_specs=in_specs, out_specs=out_specs, check_vma=False
    )
```

```python
import jax
import jax.numpy as jnp
from jax import lax
from jax.experimental import pallas as pl
from jax.experimental.pallas import tpu as pltpu
from jax.sharding import PartitionSpec as P

f32 = jnp.float32
bf16 = jnp.bfloat16

LANES = 128
GROUP = 8
SEQS = 4
BLOCKS = 32
ROWS = BLOCKS * SEQS
SIGNAL = ROWS * GROUP
TAPS = BLOCKS * LANES
WIDE = TAPS + LANES
DMIX, CONV, FGRAD = 1, 2, 8
NEAR = ((0, 0), (1, 0), (3, 0), (2, 0), (2, 1), (3, 1), (1, 1), (0, 1))
HALF = 16
SPAN = 1024


def pack_kernel(quarter_ref, weight_ref, out_ref, picks):
    @pl.when(pl.program_id(0) == 0)
    def _():
        source = lax.broadcasted_iota(jnp.int32, (SPAN, 2 * LANES), 0)
        target = lax.broadcasted_iota(jnp.int32, (SPAN, 2 * LANES), 1)
        wanted = (target % LANES // 4) * 32 + quarter_ref[0] * GROUP + (target // LANES) * 4 + target % 4
        chosen = (source == wanted).astype(f32).astype(bf16)
        for part in range(4):
            columns = weight_ref[:, part * SPAN : (part + 1) * SPAN]
            picked = jnp.dot(columns, chosen, preferred_element_type=f32).astype(bf16)
            for side in range(2):
                picks[side, :, part * LANES : (part + 1) * LANES] = picked[:, side * LANES : (side + 1) * LANES]

    count = picks.shape[1]
    for dest in range(out_ref.shape[0] // count):
        out_ref[dest * count : (dest + 1) * count, :] = picks[dest % 2]


def load_pair(pair_ref):
    both = pair_ref[...].astype(f32).reshape(ROWS, 2, GROUP, LANES)
    return both[:, 0].reshape(SIGNAL, LANES), both[:, 1].reshape(SIGNAL, LANES)


def taps_kernel(filters_ref, taps_ref, rolled):
    chan = pl.program_id(0)

    @pl.when(chan == 0)
    def _():
        padded = jnp.concatenate([filters_ref[...], jnp.zeros((GROUP, LANES), f32)], axis=1)
        for row in range(GROUP):
            turned = pltpu.roll(padded, row, 1) if row else padded
            for block in range(BLOCKS + 1):
                rolled[block, row * GROUP : (row + 1) * GROUP, :] = turned[:, block * LANES : (block + 1) * LANES]

    base = jnp.concatenate(
        [rolled[block, pl.ds(chan, GROUP, stride=GROUP), :] for block in range(BLOCKS + 1)], axis=1
    )
    for pair in range(LANES // 16):
        low = pltpu.roll(base, 16 * pair, 1) if pair else base
        high = pltpu.roll(base, 16 * pair + 8, 1)
        tile = jnp.concatenate([low[:, :TAPS], high[:, :TAPS]], axis=0).astype(bf16)
        for block in range(BLOCKS):
            taps_ref[0, block * LANES + 16 * pair : block * LANES + 16 * pair + 16, :] = tile[
                :, block * LANES : (block + 1) * LANES
            ]


def fill_ahead(grads, copies, chan):
    for part in range(SEQS):
        copies[part, 0:ROWS, :] = grads[pl.ds(part * SEQS * GROUP + chan, ROWS, stride=GROUP), :].astype(bf16)


def ahead_of(copies, block):
    return copies[block % 4, block // 4 * 16 : block // 4 * 16 + ROWS, :]


def clear_ahead(grads, copies, dconv):
    grads[0:SIGNAL, :] = dconv
    grads[SIGNAL:, :] = jnp.zeros((LANES, LANES), f32)
    for copy in copies:
        for part in range(SEQS):
            copy[part, ROWS:, :] = jnp.zeros((ROWS, LANES), bf16)


def start_taps(taps_ref, taps, done):
    for chan in range(GROUP):
        pltpu.make_async_copy(taps_ref.at[chan], taps.at[chan], done.at[chan]).start()


def wait_taps(taps_ref, taps, done, chan):
    pltpu.make_async_copy(taps_ref.at[chan], taps.at[chan], done.at[chan]).wait()


def dmix_kernel(taps_ref, skip_ref, pair_ref, dmix_ref, dvalue_ref, taps, done, grads, result, *copies):
    step = pl.program_id(0)

    @pl.when(step == 0)
    def _():
        start_taps(taps_ref, taps, done)
        clear_ahead(grads, copies, load_pair(pair_ref)[0])

    for index, copy in enumerate(copies):
        chan = step * DMIX + index
        fill_ahead(grads, copy, chan)
        ahead = jnp.concatenate([ahead_of(copy, block) for block in range(BLOCKS)], axis=1)
        wait_taps(taps_ref, taps, done, chan)
        wide = jnp.concatenate([taps[chan, block * LANES : (block + 1) * LANES, :] for block in range(BLOCKS)], axis=1)
        total = lax.dot_general(ahead, wide, (((1,), (1,)), ((), ())), preferred_element_type=f32)
        own = grads[pl.ds(chan, ROWS, stride=GROUP), :]
        result[pl.ds(chan, ROWS, stride=GROUP), :] = total + skip_ref[chan] * own

    @pl.when(step == pl.num_programs(0) - 1)
    def _():
        _, key = load_pair(pair_ref)
        dmix = result[...].astype(bf16)
        dmix_ref[...] = dmix
        dvalue = (dmix.astype(f32) * key).reshape(BLOCKS, SEQS, GROUP, LANES)
        for seq in range(SEQS):
            dvalue_ref[:, seq * LANES : (seq + 1) * LANES] = (
                dvalue[:, seq].reshape(BLOCKS * GROUP, LANES).astype(bf16)
            )


def project_kernel(column_ref, weight_ref, tokens_ref, out0, out1, out2, out3, turned):
    @pl.when(pl.program_id(0) == 0)
    def _():
        for step in range(4):
            lanes = pl.ds(pl.multiple_of((column_ref[0] + step) % 4 * LANES, LANES), LANES)
            turned[step * LANES : (step + 1) * LANES, :] = weight_ref[:, lanes].T

    product = lax.dot_general(turned[...], tokens_ref[...], (((1,), (1,)), ((), ())), preferred_element_type=f32)
    product = product.astype(bf16)
    for step, out_ref in enumerate((out0, out1, out2, out3)):
        out_ref[...] = product[step * LANES : (step + 1) * LANES, :]


def halves_of(even, odd):
    upper = lax.broadcasted_iota(jnp.int32, even.shape, 0) < 4
    return jnp.where(upper, even, pltpu.roll(odd, 4, 0)), jnp.where(upper, pltpu.roll(even, 4, 0), odd)


def join_kernel(part0, part1, part2, part3, dvalue_ref, out_ref):
    value = part0[...].astype(f32) + part1[...].astype(f32) + part2[...].astype(f32) + part3[...].astype(f32)
    value = value.astype(bf16).astype(f32)
    dvalue = dvalue_ref[...].astype(f32)
    sides = []
    for side in range(2):
        order = [NEAR.index((seq, side)) for seq in range(SEQS)]
        sides.append(jnp.concatenate([value[:, piece * LANES : (piece + 1) * LANES] for piece in order], axis=1))
    for two in range(BLOCKS // 2):
        rows = [part[two * GROUP : (two + 1) * GROUP, :] for part in sides]
        for place, tile in enumerate(halves_of(*rows)):
            index = 2 * two + place
            tile = jnp.concatenate([tile, dvalue[index * GROUP : (index + 1) * GROUP, :]], axis=0)
            out_ref[index * HALF : (index + 1) * HALF, :] = tile.astype(bf16)


def back_kernel(place_ref, dvalue_ref, own_ref, other_ref, sent_ref, kept_ref, total):
    index = pl.program_id(0)
    dvalue = dvalue_ref[...].astype(f32)
    tiles = [[], []]
    for two in range(BLOCKS // 2):
        start = two * HALF
        pair = halves_of(dvalue[start : start + GROUP, :], dvalue[start + GROUP : start + HALF, :])
        for half in range(2):
            tiles[half].append(pair[half])
    upper, lower = [jnp.concatenate(part, axis=0).astype(bf16) for part in tiles]
    first = place_ref[0] == 0
    rows = jnp.concatenate([jnp.where(first, upper, lower), jnp.where(first, lower, upper)], axis=0)
    columns = jnp.concatenate([own_ref[...], other_ref[...]], axis=1)
    term = lax.dot_general(rows, columns, (((0,), (1,)), ((), ())), preferred_element_type=f32)

    @pl.when(index == 0)
    def _():
        total[...] = term

    @pl.when(index > 0)
    def _():
        total[...] += term

    @pl.when(index == 3)
    def _():
        core = place_ref[1]
        for chip in range(2):
            rows = slice(chip * LANES, (chip + 1) * LANES)
            sent_ref[rows, :] = total[pl.ds((2 * chip + 1 - core) * LANES, LANES), :].astype(bf16)
            kept_ref[rows, :] = total[pl.ds((2 * chip + core) * LANES, LANES), :]


def middle_kernel(place_ref, kept_ref, received_ref, sent_ref, rest_ref):
    chip = place_ref[2]
    for target, index in ((sent_ref, 1 - chip), (rest_ref, chip)):
        rows = pl.ds(pl.multiple_of(index * LANES, LANES), LANES)
        target[...] = (kept_ref[rows, :] + received_ref[rows, :].astype(f32)).astype(bf16)


def order_kernel(place_ref, near_ref, far_ref, fgrad_ref, skip_ref):
    pieces = []
    for ref in (near_ref, far_ref):
        both = ref[...].astype(f32)
        pieces += [both[0 : 4 * GROUP, :], both[4 * GROUP :, :]]
    for bit, flag in ((1, place_ref[1]), (2, place_ref[2])):
        pieces = [jnp.where(flag == 0, pieces[index], pieces[index ^ bit]) for index in range(SEQS)]
    for index, piece in enumerate(pieces):
        for part in range(4):
            rows = slice(part * GROUP, (part + 1) * GROUP)
            fgrad_ref[index * GROUP : (index + 1) * GROUP, part * SPAN : (part + 1) * SPAN] = piece[rows, :]
    shape = (SEQS * GROUP, LANES)
    diagonal = lax.broadcasted_iota(jnp.int32, shape, 0) == lax.broadcasted_iota(jnp.int32, shape, 1)
    lag0 = jnp.broadcast_to(fgrad_ref[:, 0:1], shape)
    skip_ref[...] = jnp.sum(jnp.where(diagonal, lag0, 0.0), axis=0, keepdims=True)


def conv_kernel(taps_ref, skip_ref, pair_ref, value_ref, dmix_ref, out_ref, mix_ref, taps, done, mixes, values, result, *copies):
    step = pl.program_id(0)

    @pl.when(step == 0)
    def _():
        start_taps(taps_ref, taps, done)
        _, key = load_pair(pair_ref)
        value = value_ref[...].astype(f32)
        for two in range(BLOCKS // 2):
            start = two * 2 * HALF
            pair = halves_of(value[start : start + GROUP, :], value[start + HALF : start + HALF + GROUP, :])
            for side in range(2):
                for seq in range(SEQS):
                    row = ((2 * two + side) * SEQS + seq) * GROUP
                    values[row : row + GROUP, :] = pair[side][:, seq * LANES : (seq + 1) * LANES]
        mix = (key * values[...]).astype(bf16)
        mix_ref[...] = mix
        mixes[0:LANES, :] = jnp.zeros((LANES, LANES), f32)
        mixes[LANES:, :] = mix.astype(f32)
        for copy in copies:
            for part in range(SEQS):
                copy[part, 0:ROWS, :] = jnp.zeros((ROWS, LANES), bf16)

    for index, copy in enumerate(copies):
        chan = step * CONV + index
        for part in range(SEQS):
            copy[part, ROWS:, :] = mixes[
                pl.ds(LANES - part * SEQS * GROUP + chan, ROWS, stride=GROUP), :
            ].astype(bf16)
        behind = [
            copy[block % 4, ROWS - block // 4 * 16 : 2 * ROWS - block // 4 * 16, :] for block in range(BLOCKS)
        ]
        own = mixes[pl.ds(LANES + chan, ROWS, stride=GROUP), :]
        wait_taps(taps_ref, taps, done, chan)
        total = jnp.dot(jnp.concatenate(behind, axis=1), taps[chan], preferred_element_type=f32)
        result[pl.ds(chan, ROWS, stride=GROUP), :] = total + skip_ref[chan] * own

    @pl.when(step == pl.num_programs(0) - 1)
    def _():
        kgrad = dmix_ref[...].astype(f32) * values[...]
        both = [result[...].reshape(ROWS, 1, GROUP, LANES), kgrad.reshape(ROWS, 1, GROUP, LANES)]
        out_ref[...] = jnp.concatenate(both, axis=1).reshape(2 * SIGNAL, LANES).astype(bf16)


def fgrad_kernel(pair_ref, mix_ref, fgrad_ref, mixes, grads, sums, *scratch):
    step = pl.program_id(0)
    copies, corrs = scratch[:FGRAD], scratch[FGRAD:]

    @pl.when(step == 0)
    def _():
        clear_ahead(grads, copies, load_pair(pair_ref)[0])
        mixes[...] = mix_ref[...].astype(f32)
        for corr in corrs:
            corr[:, TAPS:] = jnp.zeros((LANES, LANES), f32)

    for index, (copy, corr) in enumerate(zip(copies, corrs)):
        chan = step * FGRAD + index
        fill_ahead(grads, copy, chan)
        own = mixes[pl.ds(chan, ROWS, stride=GROUP), :].T.astype(bf16)
        for block in range(0, BLOCKS, 2):
            two = jnp.concatenate([ahead_of(copy, block), ahead_of(copy, block + 1)], axis=1)
            corr[:, block * LANES : (block + 2) * LANES] = jnp.dot(own, two, preferred_element_type=f32)
    for index, corr in enumerate(corrs):
        chan = step * FGRAD + index
        acc = corr[0:GROUP, :]
        for group in range(1, LANES // GROUP):
            acc = acc + pltpu.roll(corr[group * GROUP : (group + 1) * GROUP, :], WIDE - group * GROUP, 1)
        rows = pl.ds(pl.multiple_of(chan * GROUP, GROUP), GROUP)
        for block in range(BLOCKS + 1):
            sums[block, rows, :] = acc[:, block * LANES : (block + 1) * LANES]

    @pl.when(step == pl.num_programs(0) - 1)
    def _():
        fgrad = None
        for row in range(GROUP):
            part = jnp.concatenate(
                [sums[block, pl.ds(row, GROUP, stride=GROUP), :] for block in range(BLOCKS + 1)], axis=1
            )
            fgrad = part if row == 0 else fgrad + pltpu.roll(part, WIDE - row, 1)
        parts = [fgrad[:, part * SPAN : (part + 1) * SPAN] for part in range(4)]
        fgrad_ref[...] = jnp.concatenate(parts, axis=0).astype(bf16)


def whole(shape):
    return pl.BlockSpec(shape, lambda chan: (0,) * len(shape))


params = pltpu.CompilerParams(vmem_limit_bytes=24 * 1024 * 1024)
smem = pl.BlockSpec(memory_space=pltpu.SMEM)
taps_spec = pl.BlockSpec((1, TAPS, LANES), lambda chan: (chan, 0, 0))
any_spec = pl.BlockSpec(memory_space=pl.ANY)
taps_scratch = [pltpu.VMEM((GROUP, TAPS, LANES), bf16), pltpu.SemaphoreType.DMA((GROUP,))]
pair_spec = whole((2 * SIGNAL, LANES))


def pack(quarter, weight):
    steps, rows = 4, weight.shape[0]
    return pl.pallas_call(
        pack_kernel,
        grid=(steps,),
        in_specs=[smem, pl.BlockSpec(weight.shape, lambda step: (0, 0))],
        out_specs=pl.BlockSpec((rows * BLOCKS // steps, 4 * LANES), lambda step: (step, 0)),
        out_shape=jax.ShapeDtypeStruct((rows * BLOCKS, 4 * LANES), bf16),
        scratch_shapes=[pltpu.VMEM((2, rows, 4 * LANES), bf16)],
        compiler_params=params,
        name="pack",
    )(quarter, pltpu.with_memory_space_constraint(weight, pltpu.HBM))


def build_taps(filters):
    return pl.pallas_call(
        taps_kernel,
        grid=(GROUP,),
        in_specs=[whole((GROUP, TAPS))],
        out_specs=taps_spec,
        out_shape=jax.ShapeDtypeStruct((GROUP, TAPS, LANES), bf16),
        scratch_shapes=[pltpu.VMEM((BLOCKS + 1, GROUP * GROUP, LANES), f32)],
        compiler_params=params,
        name="build_taps",
    )(filters)


def early_dmix(taps, skip, pair):
    return pl.pallas_call(
        dmix_kernel,
        grid=(GROUP // DMIX,),
        in_specs=[any_spec, smem, pair_spec],
        out_specs=[whole((SIGNAL, LANES)), whole((BLOCKS * GROUP, SEQS * LANES))],
        out_shape=[
            jax.ShapeDtypeStruct((SIGNAL, LANES), bf16),
            jax.ShapeDtypeStruct((BLOCKS * GROUP, SEQS * LANES), bf16),
        ],
        scratch_shapes=taps_scratch
        + [
            pltpu.VMEM((SIGNAL + LANES, LANES), f32),
            pltpu.VMEM((SIGNAL, LANES), f32),
        ]
        + [pltpu.VMEM((SEQS, 2 * ROWS, LANES), bf16)] * DMIX,
        compiler_params=params,
        name="early_dmix",
    )(pltpu.with_memory_space_constraint(taps, pltpu.HBM), skip, pair)


def project(column, weight, tokens):
    count, steps = tokens.shape[0], 4
    return pl.pallas_call(
        project_kernel,
        grid=(steps,),
        in_specs=[smem, whole(weight.shape), pl.BlockSpec((count // steps, SPAN), lambda step: (step, 0))],
        out_specs=[pl.BlockSpec((LANES, count // steps), lambda step: (0, step))] * 4,
        out_shape=[jax.ShapeDtypeStruct((LANES, count), bf16)] * 4,
        scratch_shapes=[pltpu.VMEM((4 * LANES, SPAN), bf16)],
        compiler_params=params,
        name="project",
    )(column, *[pltpu.with_memory_space_constraint(x, pltpu.HBM) for x in (weight, tokens)])


def vmem_specs(count):
    return [smem] + [pl.BlockSpec(memory_space=pltpu.VMEM)] * count


def join(parts, dvalue):
    return pl.pallas_call(
        join_kernel,
        out_shape=jax.ShapeDtypeStruct((BLOCKS * HALF, SEQS * LANES), bf16),
        compiler_params=params,
        name="join",
    )(*parts, dvalue)


def back(place, dvalue, own, other):
    return pl.pallas_call(
        back_kernel,
        grid=(4,),
        in_specs=[
            smem,
            pl.BlockSpec((BLOCKS * GROUP, SEQS * LANES), lambda step: (step, 0)),
            pl.BlockSpec((SPAN, LANES), lambda step: (0, step)),
            pl.BlockSpec((SPAN, LANES), lambda step: (0, step)),
        ],
        out_specs=[whole((2 * LANES, SPAN)), whole((2 * LANES, SPAN))],
        out_shape=[
            jax.ShapeDtypeStruct((2 * LANES, SPAN), bf16),
            jax.ShapeDtypeStruct((2 * LANES, SPAN), f32),
        ],
        scratch_shapes=[pltpu.VMEM((SEQS * LANES, SPAN), f32)],
        compiler_params=params,
        name="back",
    )(place, *[pltpu.with_memory_space_constraint(x, pltpu.HBM) for x in (dvalue, own, other)])


def middle(place, kept, received):
    return pl.pallas_call(
        middle_kernel,
        in_specs=vmem_specs(2),
        out_shape=[jax.ShapeDtypeStruct((LANES, SPAN), bf16)] * 2,
        compiler_params=params,
        name="middle",
    )(place, kept, received)


def order(place, near, far):
    return pl.pallas_call(
        order_kernel,
        in_specs=vmem_specs(2),
        out_shape=[jax.ShapeDtypeStruct((SEQS * GROUP, TAPS), f32), jax.ShapeDtypeStruct((1, LANES), f32)],
        compiler_params=params,
        name="order",
    )(place, near, far)


def late_conv(taps, skip, pair, value, dmix):
    return pl.pallas_call(
        conv_kernel,
        grid=(GROUP // CONV,),
        in_specs=[
            any_spec,
            smem,
            pair_spec,
            whole((BLOCKS * HALF, SEQS * LANES)),
            whole((SIGNAL, LANES)),
        ],
        out_specs=[whole((2 * SIGNAL, LANES)), whole((SIGNAL, LANES))],
        out_shape=[
            jax.ShapeDtypeStruct((2 * SIGNAL, LANES), bf16),
            jax.ShapeDtypeStruct((SIGNAL, LANES), bf16),
        ],
        scratch_shapes=taps_scratch
        + [
            pltpu.VMEM((SIGNAL + LANES, LANES), f32),
            pltpu.VMEM((SIGNAL, LANES), f32),
            pltpu.VMEM((SIGNAL, LANES), f32),
        ]
        + [pltpu.VMEM((SEQS, 2 * ROWS, LANES), bf16)] * CONV,
        compiler_params=params,
        name="late_conv",
    )(pltpu.with_memory_space_constraint(taps, pltpu.HBM), skip, pair, value, dmix)


def late_fgrad(pair, mix):
    return pl.pallas_call(
        fgrad_kernel,
        grid=(GROUP // FGRAD,),
        in_specs=[pair_spec, whole((SIGNAL, LANES))],
        out_specs=whole((4 * GROUP, SPAN)),
        out_shape=jax.ShapeDtypeStruct((4 * GROUP, SPAN), bf16),
        scratch_shapes=[
            pltpu.VMEM((SIGNAL, LANES), f32),
            pltpu.VMEM((SIGNAL + LANES, LANES), f32),
            pltpu.VMEM((BLOCKS + 1, GROUP * GROUP, LANES), f32),
        ]
        + [pltpu.VMEM((SEQS, 2 * ROWS, LANES), bf16)] * FGRAD
        + [pltpu.VMEM((LANES, WIDE), f32)] * FGRAD,
        compiler_params=params,
        name="late_fgrad",
    )(pair, mix)


def swap(values, axes, groups=None):
    return lax.all_to_all(values, axes, split_axis=0, concat_axis=0, tiled=True, axis_index_groups=groups)


def per_device(inputs, value_weight, query, key, filters, skip, cotangent):
    quarter = lax.axis_index("dp")
    side = lax.axis_index("context") % 2

    place = jnp.stack([side, quarter % 2, quarter // 2]).astype(jnp.int32)

    near = [[seq * BLOCKS + 2 * k + place for seq, place in NEAR] for k in range(BLOCKS // 2)]
    tokens = lax.all_gather(inputs[0], ("dp", "context"), axis=0, tiled=True, axis_index_groups=near)
    own_filters = lax.dynamic_slice_in_dim(filters, quarter * GROUP, GROUP, 0)
    own_skip = lax.dynamic_slice_in_dim(skip, quarter * GROUP, GROUP, 0)
    taps = build_taps(own_filters)

    packed = pack(quarter.astype(jnp.int32)[None], value_weight)
    weight = swap(packed.reshape(BLOCKS, value_weight.shape[0], 4 * LANES), "context").reshape(SPAN, 4 * LANES)

    query_part = query[0].astype(f32)
    upstream = cotangent[0].astype(f32)
    dconv = (upstream * query_part).astype(bf16)
    pair = jnp.concatenate([dconv.reshape(ROWS, 1, GROUP, LANES), key[0].reshape(ROWS, 1, GROUP, LANES)], axis=1)
    pair, weight, taps = lax.optimization_barrier((pair, weight, taps))
    pair = swap(pair, ("context", "dp")).reshape(2 * SIGNAL, LANES)

    column = lax.axis_index("tensor").astype(jnp.int32)[None]
    parts = project(column, weight, tokens)
    parts = [parts[0]] + [
        lax.ppermute(parts[step], "tensor", [(i, (i + step) % 4) for i in range(4)]) for step in (1, 2, 3)
    ]
    other = lax.ppermute(weight, "context", [(k, k ^ 1) for k in range(BLOCKS)])
    dmix, dvalue = early_dmix(taps, own_skip, pair)

    both = swap(join(parts, dvalue).reshape(BLOCKS, HALF, SEQS * LANES), "context")
    both, other = lax.optimization_barrier((both, other))
    dvalue = lax.all_gather(both[:, GROUP:].reshape(BLOCKS * GROUP, SEQS * LANES), "tensor", axis=0, tiled=True)
    out, mix = late_conv(taps, own_skip, pair, both.reshape(BLOCKS * HALF, SEQS * LANES), dmix)
    out = swap(out.reshape(ROWS, 2, GROUP, LANES), ("context", "dp"))
    fgrad = late_fgrad(pair, mix)

    def cross(values, bit):
        return lax.ppermute(values, "dp", [(i, i ^ bit) for i in range(SEQS)])

    place = jnp.stack([side, quarter % 2, quarter // 2]).astype(jnp.int32)
    chip_fgrads = jnp.concatenate([fgrad, cross(fgrad, 1)], axis=0)
    far_fgrads = cross(chip_fgrads, 2)
    dvalue, chip_fgrads = lax.optimization_barrier((dvalue, chip_fgrads))
    sent, kept = back(place, dvalue, weight, other)
    sent, rest = middle(place, kept, cross(sent, 1))
    sent, rest, out, chip_fgrads = lax.optimization_barrier((sent, rest, out, chip_fgrads))
    input_grad = (rest.astype(f32) + cross(sent, 2).astype(f32)).astype(bf16)
    filter_grad, skip_grad = order(place, chip_fgrads, far_fgrads)
    skip_grad = skip_grad[0, : skip.shape[0]]

    conv = out[:, 0].reshape(SIGNAL, LANES).astype(f32)
    key_grad = out[:, 1].reshape(SIGNAL, LANES)
    gated = (query_part * conv).astype(bf16)
    query_grad = (upstream * conv).astype(bf16)
    return (gated[None], query_grad[None], key_grad[None], input_grad[None], filter_grad, skip_grad)


def solution(mesh):
    by_channel = P("dp", "tensor", "context")
    by_row = P(("tensor", "context"), None)
    in_specs = (
        P("dp", "context", "tensor"),
        by_row,
        by_channel,
        by_channel,
        by_row,
        P(("tensor", "context")),
        by_channel,
    )
    out_specs = (
        by_channel,
        by_channel,
        by_channel,
        P("dp", "context", "tensor"),
        by_row,
        P(("tensor", "context")),
    )
    return jax.shard_map(
        per_device, mesh=mesh, in_specs=in_specs, out_specs=out_specs, check_vma=False
    )
```
